256 devices in a mesh: dp: 8 (over y, z_hi), tensor: 32 (over x, z_lo, core).
Axes of the slice: x: 4, y: 4, z: 8 (z_hi: 2, z_lo: 4; z = z_hi * 4 + z_lo), core: 2. Of those that a mesh axis runs over, the one named last changes fastest.
Arguments:
- tokens: bfloat16 [1024, 16384], P('dp', 'tensor'), may hold values from -6 to 6
- mixed: bfloat16 [1024, 16384], P('dp', 'tensor'), may hold values from -6 to 6
- angles: float32 [4, 5, 8192], replicated, may hold values from -1 to 1
- q_packed: float32 [4096, 8192], P('tensor'), may hold values from 0 to 65535, as said below
- q_scale: bfloat16 [256, 8192], P('tensor'), may hold values from 0.0007972717 to 0.003189087
- k_packed: float32 [4096, 1024], P('tensor'), may hold values from 0 to 65535, as said below
- k_scale: bfloat16 [256, 1024], P('tensor'), may hold values from 0.0007972717 to 0.003189087
- v_packed: float32 [4096, 1024], P('tensor'), may hold values from 0 to 65535, as said below
- v_scale: bfloat16 [256, 1024], P('tensor'), may hold values from 0.0007972717 to 0.003189087
- o_packed: float32 [4096, 8192], P('tensor'), may hold values from 0 to 65535, as said below
- o_scale: bfloat16 [256, 8192], P('tensor'), may hold values from 0.0007972717 to 0.003189087
- q_cot: bfloat16 [1024, 8192], P('dp', 'tensor'), may hold values from -1.5 to 1.5
- k_cot: bfloat16 [1024, 1024], P('dp', 'tensor'), may hold values from -6 to 6
- v_cot: bfloat16 [1024, 1024], P('dp', 'tensor'), may hold values from -6 to 6
- o_cot: bfloat16 [1024, 8192], P('dp', 'tensor'), may hold values from -1.5 to 1.5
Outputs:
- q_out: bfloat16 [1024, 8192], P('dp', 'tensor')
- k_out: bfloat16 [1024, 1024], P('dp', 'tensor')
- v_out: bfloat16 [1024, 1024], P('dp', 'tensor')
- o_out: bfloat16 [1024, 8192], P('dp', 'tensor')
- token_grad: bfloat16 [1024, 16384], P('dp', 'tensor')
- mixed_grad: bfloat16 [1024, 16384], P('dp', 'tensor')
- angle_grad: float32 [4, 5, 16384], P(None, None, 'tensor')
The draws below stay inside these ranges and needn't reach their ends.
Inputs may be any that keep to these rules, and one draw needn't show every extreme that they name: `q_packed`: each entry is a whole number; it holds the 4-bit codes of four consecutive input rows, row 4 w + i in base-16 digit i of entry w. `k_packed`: packed as q_packed. `v_packed`: packed as q_packed. `o_packed`: packed as q_packed.
All inputs are finite; a program needn't handle non-finite values.
Results may differ from the reference program's by a relative error of at most 0.034.
Values may be sent and summed in bfloat16 or wider, within the bound.
A program may use at most 320 MiB of HBM per device.

```python
import math
import jax
import jax.numpy as jnp
from jax import lax

D = 16384
KVD = 1024
OUTW = 8192
GROUP = 64
SECTIONS = 5
TOKENS = 1024
PAIRS = 8192
N_TENSOR = 32


def draw_q_packed(key, part):
    key = jax.random.fold_in(key, 11)
    return jax.random.randint(key, (D // 4, OUTW), 0, 65536).astype(jnp.float32)


def draw_k_packed(key, part):
    key = jax.random.fold_in(key, 12)
    return jax.random.randint(key, (D // 4, KVD), 0, 65536).astype(jnp.float32)


def draw_v_packed(key, part):
    key = jax.random.fold_in(key, 13)
    return jax.random.randint(key, (D // 4, KVD), 0, 65536).astype(jnp.float32)


def draw_o_packed(key, part):
    key = jax.random.fold_in(key, 14)
    return jax.random.randint(key, (D // 4, OUTW), 0, 65536).astype(jnp.float32)


def shard_levels(rng, dims, cuts, least, top_value):
    def one(axis_at, parts):
        draws = jax.random.uniform(jax.random.fold_in(jax.random.fold_in(rng, 6), axis_at), (parts,), jnp.float32, least / len(cuts), top_value / len(cuts))
        return jnp.repeat(jnp.exp(draws), dims[axis_at] // parts).reshape((-1,) + (1,) * (len(dims) - axis_at - 1))

    gain = one(*cuts[0])
    for cut in cuts[1:]:
        gain = gain * one(*cut)
    return gain


def noise(key, dims, deviation, bound, cuts=(), kind=jnp.bfloat16):
    values = deviation * jax.random.normal(key, dims, jnp.float32)
    if cuts:
        values = values * shard_levels(key, dims, cuts, -0.22, 0.18)
    return jnp.clip(values, -bound, bound).astype(kind)


def setup_inputs(seed: int = 0) -> dict:
    seeds = jax.random.split(jax.random.key(seed), 16)
    return {
        "tokens": noise(seeds[0], (TOKENS, D), 1.0, 6.0, ((0, 8), (1, 32))),
        "mixed": noise(seeds[1], (TOKENS, D), 1.0, 6.0, ((0, 8), (1, 32))),
        "angles": jnp.clip(jax.random.uniform(seeds[2], (4, SECTIONS, PAIRS), jnp.float32, -1.0, 1.0), -1.0, 1.0),
        "q_packed": draw_q_packed(jax.random.fold_in(seeds[15], 71), 0),
        "q_scale": jnp.clip(jnp.exp(math.log(0.003189087) - 1.3862944 * jax.random.uniform(seeds[4], (D // GROUP, OUTW), jnp.float32) ** shard_levels(seeds[4], (D // GROUP, OUTW), ((0, 32),), -0.2, 0.2)), 0.0007972717, 0.003189087).astype(jnp.bfloat16),
        "k_packed": draw_k_packed(jax.random.fold_in(seeds[15], 71), 0),
        "k_scale": jnp.clip(jnp.exp(math.log(0.003189087) - 1.3862944 * jax.random.uniform(seeds[6], (D // GROUP, KVD), jnp.float32) ** shard_levels(seeds[6], (D // GROUP, KVD), ((0, 32),), -0.2, 0.2)), 0.0007972717, 0.003189087).astype(jnp.bfloat16),
        "v_packed": draw_v_packed(jax.random.fold_in(seeds[15], 71), 0),
        "v_scale": jnp.clip(jnp.exp(math.log(0.003189087) - 1.3862944 * jax.random.uniform(seeds[8], (D // GROUP, KVD), jnp.float32) ** shard_levels(seeds[8], (D // GROUP, KVD), ((0, 32),), -0.2, 0.2)), 0.0007972717, 0.003189087).astype(jnp.bfloat16),
        "o_packed": draw_o_packed(jax.random.fold_in(seeds[15], 71), 0),
        "o_scale": jnp.clip(jnp.exp(math.log(0.003189087) - 1.3862944 * jax.random.uniform(seeds[10], (D // GROUP, OUTW), jnp.float32) ** shard_levels(seeds[10], (D // GROUP, OUTW), ((0, 32),), -0.2, 0.2)), 0.0007972717, 0.003189087).astype(jnp.bfloat16),
        "q_cot": noise(seeds[11], (TOKENS, OUTW), 0.25, 1.5, ((0, 8), (1, 32))),
        "k_cot": noise(seeds[12], (TOKENS, KVD), 1.0, 6.0, ((0, 8), (1, 32))),
        "v_cot": noise(seeds[13], (TOKENS, KVD), 1.0, 6.0, ((0, 8), (1, 32))),
        "o_cot": noise(seeds[14], (TOKENS, OUTW), 0.25, 1.5, ((0, 8), (1, 32))),
    }


def dequantize(packed, scale):
    inverse = jnp.array([1.0, 0.0625, 0.00390625, 0.000244140625], dtype=jnp.float32)[None, :, None]
    scaled = packed[:, None, :] * inverse
    digit = jnp.floor(scaled) - 16.0 * jnp.floor(scaled * 0.0625)
    row_count = packed.shape[0] * 4
    levels = digit.reshape(row_count, packed.shape[1]) - 7.5
    spread = jnp.repeat(scale.astype(jnp.float32), row_count // scale.shape[0], axis=0)
    return (levels * spread).astype(jnp.bfloat16)


def rotation(angle):
    square = angle * angle
    denominator = 1.0 + square
    return (1.0 - square) / denominator, 2.0 * angle / denominator


def rotation_slope(angle):
    square = angle * angle
    denominator = (1.0 + square) * (1.0 + square)
    return -4.0 * angle / denominator, 2.0 * (1.0 - square) / denominator


def split_pair(values, section_bit):
    blocks = values.reshape(values.shape[0], values.shape[1] >> (section_bit + 1), 2, 1 << section_bit)
    return blocks[:, :, 0], blocks[:, :, 1]


def rotate_forward(hidden, chain_angles):
    log_width = D.bit_length() - 1
    states = []
    for section_num in range(SECTIONS):
        section_bit = log_width - 1 - section_num
        states.append(hidden)
        lower, upper = split_pair(hidden.astype(jnp.float32), section_bit)
        angle = chain_angles[section_num].reshape(lower.shape[1], lower.shape[2])
        cosine, sine = rotation(angle)
        joined = jnp.stack([cosine * lower - sine * upper, sine * lower + cosine * upper], axis=2)
        hidden = joined.reshape(hidden.shape).astype(jnp.bfloat16)
    return hidden, states


def rotate_backward(cotangent, states, chain_angles):
    log_width = D.bit_length() - 1
    grads = []
    for section_num in reversed(range(SECTIONS)):
        section_bit = log_width - 1 - section_num
        lower, upper = split_pair(states[section_num].astype(jnp.float32), section_bit)
        grad_lower, grad_upper = split_pair(cotangent.astype(jnp.float32), section_bit)
        angle = chain_angles[section_num].reshape(lower.shape[1], lower.shape[2])
        cosine, sine = rotation(angle)
        cos_slope, sin_slope = rotation_slope(angle)
        direct = jnp.sum(grad_lower * lower + grad_upper * upper, axis=0)
        crossed = jnp.sum(grad_upper * lower - grad_lower * upper, axis=0)
        pair_grad = direct * cos_slope + crossed * sin_slope
        grads.insert(0, jnp.stack([pair_grad, pair_grad], axis=1).reshape(D))
        joined = jnp.stack([cosine * grad_lower + sine * grad_upper, cosine * grad_upper - sine * grad_lower], axis=2)
        result = joined.reshape(cotangent.shape)
        cotangent = result if section_num == 0 else result.astype(jnp.bfloat16)
    return cotangent, jnp.stack(grads)


def row_parallel(hidden, weight):
    act_shards = hidden.reshape(hidden.shape[0], N_TENSOR, -1).transpose(1, 0, 2)
    weight_shards = weight.reshape(N_TENSOR, -1, weight.shape[1])

    def accumulate(running, pieces):
        partial_value = jnp.dot(pieces[0], pieces[1], preferred_element_type=jnp.float32)
        rounded = lax.optimization_barrier(partial_value.astype(jnp.bfloat16))
        return running + rounded.astype(jnp.float32), None

    init = jnp.zeros((hidden.shape[0], weight.shape[1]), jnp.float32)
    running, _ = lax.scan(accumulate, init, (act_shards, weight_shards))
    return running.astype(jnp.bfloat16)


def reference(tokens, mixed, angles, q_packed, q_scale, k_packed, k_scale, v_packed, v_scale, o_packed, o_scale, q_cot, k_cot, v_cot, o_cot):
    packs = [(q_packed, q_scale), (k_packed, k_scale), (v_packed, v_scale), (o_packed, o_scale)]
    inputs = [tokens, tokens, tokens, mixed]
    cotangents = [q_cot, k_cot, v_cot, o_cot]
    results = []
    input_grads = []
    chain_grads = []
    for chain_num in range(4):
        weight = dequantize(packs[chain_num][0], packs[chain_num][1])
        rotated, states = rotate_forward(inputs[chain_num], angles[chain_num])
        results.append(row_parallel(rotated, weight))
        back = jnp.dot(cotangents[chain_num], weight.T, preferred_element_type=jnp.float32).astype(jnp.bfloat16)
        input_grad, angle_part = rotate_backward(back, states, angles[chain_num])
        input_grads.append(input_grad)
        chain_grads.append(angle_part)
    token_grad = (input_grads[0] + input_grads[1] + input_grads[2]).astype(jnp.bfloat16)
    mixed_grad = input_grads[3].astype(jnp.bfloat16)
    return (results[0], results[1], results[2], results[3], token_grad, mixed_grad, jnp.stack(chain_grads))
```

```python
import jax
import jax.numpy as jnp
from jax import lax
from jax.experimental import pallas as pl
from jax.experimental.pallas import tpu as pltpu
from jax.sharding import PartitionSpec as P

F32 = jnp.float32
BF16 = jnp.bfloat16
MESH = pl.DeviceIdType.MESH
N = 32
DP = 8
CH = 512
SUB = 16
TOK = 128
SEC = 5
ROWS = 576
HALF = 288
NT = (((1,), (1,)), ((), ()))


def dot(a, b):
    return jnp.dot(a, b, preferred_element_type=F32)


def dot_nt(a, b):
    return lax.dot_general(a, b, NT, preferred_element_type=F32)


def eye(n):
    r = lax.broadcasted_iota(jnp.int32, (n, n), 0)
    c = lax.broadcasted_iota(jnp.int32, (n, n), 1)
    return jnp.where(r == c, 1.0, 0.0).astype(BF16)


def loop(lo, hi, fn, unroll=1):
    def step(i, carry):
        fn(i)
        return carry

    lax.fori_loop(lo, hi, step, 0, unroll=unroll)


def dequantize(packed, scale, out, width):
    def chunk(i):
        cols = pl.ds(pl.multiple_of(i * 128, 128), 128)
        spread = scale[:, cols].astype(F32)
        for g in range(8):
            rows = slice(16 * g, 16 * g + 16)
            word = packed[rows, cols].astype(jnp.int32)
            s = jnp.broadcast_to(spread[g : g + 1, :], (16, 128))
            for plane in range(4):
                digit = (word >> (4 * plane)) & 15 if plane < 3 else word >> 12
                value = (digit.astype(F32) - 7.5) * s
                out[128 * plane + 16 * g : 128 * plane + 16 * g + 16, cols] = value.astype(BF16)

    loop(0, width // 128, chunk)


def add_rows(dst, base, rows, srcs, out=None, out_base=0):
    def step(i):
        off = pl.multiple_of(i * 96, 96)
        total = dst[base, pl.ds(rows[0] + off, 96), :].astype(F32)
        for ref, index, first in srcs:
            total = total + ref[index + (pl.ds(first + off, 96), slice(None))].astype(F32)
        if out is None:
            dst[base, pl.ds(rows[0] + off, 96), :] = total.astype(BF16)
        else:
            out[out_base, pl.ds(rows[0] + off, 96), :] = total.astype(BF16)

    loop(0, (rows[1] - rows[0]) // 96, step)


def kernel(
    tok, mix, ang, qp, qs, kp, ks, vp, vs, op, os_, qc, kc, vc, oc,
    q_out, k_out, v_out, o_out, tg, mg, ang_out,
    packq, packk, packv, packo, wq, wk, wv, wo, perm,
    tok_t, hin, st, h5s, h5t, hl, ccos, csin,
    ag, part, ra, rx1, rx2, accx, rz, acc, kvt, bks, bkr, gs, gt, angbuf, angd,
    ld, s1, r1, s2, r2, s3, r3, s4, r4, ag_s, ag_r, ag_sib, ra_s, ra_r, rx1_s, rx1_r,
    rx2_s, rx2_r, rz_s, rz_r, sd, rd,
):
    d = lax.axis_index("dp")
    t = lax.axis_index("tensor")
    x = lax.div(t, 8)
    z = lax.rem(lax.div(t, 2), 4)
    c = lax.rem(t, 2)
    xp, xm, x2 = lax.rem(x + 1, 4), lax.rem(x + 3, 4), lax.rem(x + 2, 4)

    def dev(x_, z_, c_):
        return (x_ * 4 + z_) * 2 + c_

    sib = dev(x, z, 1 - c)

    def send(src, dst, ssem, rsem, peer, axis="tensor"):
        return pltpu.make_async_remote_copy(
            src_ref=src, dst_ref=dst, send_sem=ssem, recv_sem=rsem,
            device_id={axis: peer}, device_id_type=MESH,
        )

    loads = [
        pltpu.make_async_copy(src, dst, ld.at[i])
        for i, (src, dst) in enumerate(((kp, packk), (vp, packv), (qp, packq), (op, packo)))
    ]
    for load in loads:
        load.start()
    bar = pltpu.get_barrier_semaphore()
    loop(1, N, lambda i: pl.semaphore_signal(
        bar, inc=1, device_id={"tensor": lax.rem(t + i, N)}, device_id_type=MESH))
    loop(1, DP, lambda i: pl.semaphore_signal(
        bar, inc=1, device_id={"dp": lax.rem(d + i, DP)}, device_id_type=MESH))

    r = lax.broadcasted_iota(jnp.int32, (CH, CH), 0)
    col = lax.broadcasted_iota(jnp.int32, (CH, CH), 1)
    perm[...] = jnp.where(col == 4 * (r & 127) + (r >> 7), 1.0, 0.0).astype(BF16)
    tok_t[0] = dot_nt(perm[...], tok[...]).astype(BF16)
    tok_t[1] = dot_nt(perm[...], mix[...]).astype(BF16)
    own = c * 16 + x * 4 + z
    ag[own, 0:256, :] = dot_nt(eye(256), qc[...]).astype(BF16)
    ag[own, 256:512, :] = dot_nt(eye(256), oc[...]).astype(BF16)
    ag[own, 512:544, :] = dot_nt(eye(32), kc[...]).astype(BF16)
    ag[own, 544:576, :] = dot_nt(eye(32), vc[...]).astype(BF16)
    pl.semaphore_wait(bar, N - 1 + DP - 1)

    def mine(p):
        return pl.ds(pl.multiple_of(p * SUB, SUB), SUB)

    def in_copy(p, slot):
        return send(tok_t.at[:, mine(p), :], hin.at[slot], s1.at[p], r1.at[slot], p)

    loop(1, N, lambda i: in_copy(lax.rem(t + i, N), t).start())
    hin[t] = tok_t[:, mine(t), :]

    def ag_copy(k, x_, z_, peer, sems):
        slot = c * 16 + x_ * 4 + z_
        return send(ag.at[slot], ag.at[slot], ag_s.at[k], sems.at[x_ * 4 + z_], peer)

    def ag_wait(x_, z_, sems):
        slot = c * 16 + x_ * 4 + z_
        send(ag.at[slot], ag.at[slot], ag_s.at[0], sems.at[x_ * 4 + z_], sib).wait_recv()

    def zrel(dz):
        return lax.rem(z + dz, 4)

    for dz in (1, 2, 3):
        ag_copy(dz - 1, x, z, dev(x, zrel(dz), c), ag_r).start()

    def ag_row(dz):
        ag_copy(3 + 2 * dz, x, zrel(dz), dev(xp, z, c), ag_r).start()
        ag_copy(4 + 2 * dz, x, zrel(dz), dev(xm, z, c), ag_r).start()
        ag_copy(15 + dz, x, zrel(dz), sib, ag_sib).start()

    ag_row(0)

    lanes = lax.broadcasted_iota(jnp.int32, (SUB, TOK), 1)
    subs = lax.broadcasted_iota(jnp.int32, (SUB, TOK), 0)
    pick = lanes == 4 * subs + (64 * c + x)
    window = 128 * lax.div(lax.rem(t, 8), 2)

    def factors(pr):
        where = pl.ds(pl.multiple_of(pr * CH + window, 128), 128)
        for j in range(4):
            for n in range(SEC):
                row = jnp.broadcast_to(ang[j, n : n + 1, where], (SUB, TOK))
                angle = jnp.sum(jnp.where(pick, row, 0.0), axis=1, keepdims=True)
                square = angle * angle
                inverse = 1.0 / (1.0 + square)
                ccos[n, pr, j] = jnp.broadcast_to((1.0 - square) * inverse, (SUB, TOK))
                csin[n, pr, j] = jnp.broadcast_to(2.0 * angle * inverse, (SUB, TOK))

    loop(0, 16, factors)
    loads[0].wait()
    dequantize(packk, ks, wk, 1024)
    loads[1].wait()
    dequantize(packv, vs, wv, 1024)

    def wait_in(i):
        p = lax.rem(t + i, N)
        in_copy(p, p).wait_recv()

    loop(1, N, wait_in)

    def pair_of(n, pr):
        sh = 4 - n
        low = ((pr >> sh) << (sh + 1)) + (pr & ((1 << sh) - 1))
        return low, low + (1 << sh)

    def state(n, blk, j):
        if n == 0:
            return hin[blk, 0 if j < 3 else 1].astype(F32)
        return st[n - 1, blk, j].astype(F32)

    for n in range(SEC):

        def forward(pr, n=n):
            t0, t1 = pair_of(n, pr)
            for j in range(4):
                a, b = state(n, t0, j), state(n, t1, j)
                cs, sn = ccos[n, pr, j], csin[n, pr, j]
                low = (cs * a - sn * b).astype(BF16)
                high = (sn * a + cs * b).astype(BF16)
                if n < SEC - 1:
                    st[n, t0, j] = low
                    st[n, t1, j] = high
                else:
                    h5s[t0, j] = low
                    h5s[t1, j] = high

        loop(0, 16, forward)

    def h5_copy(p, src):
        return send(h5s.at[p], h5t.at[:, mine(src), :], s2.at[p], r2.at[src], p)

    loop(1, N, lambda i: h5_copy(lax.rem(t + i, N), t).start())
    h5t[:, mine(t), :] = h5s[t]

    for dz in (1, 2, 3):
        ag_wait(x, zrel(dz), ag_r)
        ag_row(dz)
    loads[2].wait()
    dequantize(packq, qs, wq, 8192)
    for dz in range(4):
        ag_wait(xm, zrel(dz), ag_r)
        if dz % 2 == 0:
            ag_copy(11 + dz // 2, xm, zrel(dz), dev(xp, z, c), ag_r).start()
        ag_copy(19 + dz, xm, zrel(dz), sib, ag_sib).start()
        ag_wait(xp, zrel(dz), ag_r)
        if dz % 2 == 1:
            ag_copy(13 + dz // 2, xp, zrel(dz), dev(xm, z, c), ag_r).start()
        ag_copy(23 + dz, xp, zrel(dz), sib, ag_sib).start()
    loads[3].wait()
    dequantize(packo, os_, wo, 8192)
    for dz in range(4):
        ag_wait(x2, zrel(dz), ag_r)
        ag_copy(27 + dz, x2, zrel(dz), sib, ag_sib).start()

    def wait_h5(i):
        p = lax.rem(t + i, N)
        h5_copy(p, p).wait_recv()

    loop(1, N, wait_h5)
    for j in range(4):
        hl[j] = dot_nt(eye(TOK), h5t[j]).astype(BF16)
    for j, w, first in ((1, wk, 512), (2, wv, 544)):

        def narrow(i, j=j, w=w, first=first):
            cols = pl.ds(pl.multiple_of(i * 128, 128), 128)
            piece = dot(hl[j], w[:, cols]).astype(BF16)
            turned = dot_nt(eye(TOK), piece).astype(BF16)
            for k in range(4):
                z_ = 2 * lax.rem(i, 2) + k // 2
                slot = ((k % 2) * 4 + z_) * 4 + lax.div(i, 2)
                part[slot, first : first + 32, :] = turned[32 * k : 32 * k + 32, :]

        loop(0, 8, narrow)

    def wide(zp):
        def column(x_):
            cols = pl.ds(pl.multiple_of((x_ * 4 + zp) * 512, 512), 512)
            for j, w, first in ((0, wq, 0), (3, wo, 256)):
                piece = dot(hl[j], w[:, cols]).astype(BF16)
                for c_ in range(2):
                    for half in range(2):
                        at = c_ * 256 + half * 128
                        rows = slice(first + half * 128, first + half * 128 + 128)
                        part[(c_ * 4 + zp) * 4 + x_, rows, :] = piece[:, at : at + 128]

        loop(0, 4, column)

    def piece_z(p):
        return lax.rem(z + 1 + p, 4)

    def base(zp):
        return (c * 4 + zp) * 4

    def a_copy(p):
        zp = piece_z(p)
        return send(
            part.at[pl.ds(((1 - c) * 4 + zp) * 4, 4)], ra.at[pl.ds(zp * 4, 4)],
            ra_s.at[p], ra_r.at[p], sib,
        )

    def x1_copy(p, way):
        zp = piece_z(p)
        return send(
            part.at[base(zp) + x2, pl.ds(way * HALF, HALF), :], rx1.at[zp, way],
            rx1_s.at[2 * p + way], rx1_r.at[2 * p + way], dev(xm if way else xp, z, c),
        )

    def x2_copy(p, way):
        zp = piece_z(p)
        to = xm if way else xp
        return send(
            part.at[base(zp) + to], rx2.at[zp, way],
            rx2_s.at[2 * p + way], rx2_r.at[2 * p + way], dev(to, z, c),
        )

    def z_copy(p, src):
        zp = piece_z(p)
        return send(accx.at[zp], rz.at[src], rz_s.at[p], rz_r.at[src], dev(x, zp, c))

    def stage_x1(p):
        zp = piece_z(p)
        a_copy(p).wait_recv()
        add_rows(part, base(zp) + x2, (0, ROWS), [(ra, (zp * 4 + x2,), 0)])
        x1_copy(p, 0).start()
        x1_copy(p, 1).start()
        for x_ in (xp, xm, x):
            add_rows(part, base(zp) + x_, (0, ROWS), [(ra, (zp * 4 + x_,), 0)])

    def stage_x2(p):
        zp = piece_z(p)
        x1_copy(p, 0).wait_recv()
        add_rows(part, base(zp) + xp, (0, HALF), [(rx1, (zp, 0), 0)])
        x2_copy(p, 0).start()
        x1_copy(p, 1).wait_recv()
        add_rows(part, base(zp) + xm, (HALF, ROWS), [(rx1, (zp, 1), 0)])
        x2_copy(p, 1).start()

    def stage_x3(p):
        zp = piece_z(p)
        x2_copy(p, 0).wait_recv()
        x2_copy(p, 1).wait_recv()
        add_rows(part, base(zp) + x, (0, ROWS), [(rx2, (zp, 0), 0), (rx2, (zp, 1), 0)], accx, zp)
        if p < 3:
            z_copy(p, z).start()

    for p in range(4):
        wide(piece_z(p))
        a_copy(p).start()
        if p:
            stage_x1(p - 1)
    stage_x1(3)

    for x_ in range(4):
        for z_ in range(4):
            slot = (1 - c) * 16 + x_ * 4 + z_
            send(
                ag.at[slot], ag.at[slot], ag_s.at[0], ag_sib.at[x_ * 4 + z_], sib
            ).wait_recv()

    def back_wide(j, w, first):
        acc[...] = jnp.zeros_like(acc)

        def step(i):
            rhs = jnp.concatenate(
                [ag[i, first : first + 256, :], ag[16 + i, first : first + 256, :]], axis=0
            )
            acc[...] += dot(w[:, pl.ds(pl.multiple_of(i * 512, 512), 512)], rhs)

        loop(0, 16, step)
        bks[j] = acc[...].astype(BF16)

    def back_narrow(j, w, first):
        def turn(i):
            for c_ in range(2):
                kvt[pl.ds(pl.multiple_of(i * 64 + c_ * 32, 32), 32), :] = ag[
                    c_ * 16 + i, first : first + 32, :
                ]

        loop(0, 16, turn)
        bks[j] = dot(w[...], kvt[...]).astype(BF16)

    back_wide(0, wq, 0)
    stage_x2(0)
    back_narrow(1, wk, 512)
    back_narrow(2, wv, 544)
    stage_x2(1)
    back_wide(3, wo, 256)
    stage_x2(2)

    def back_copy(p, slot):
        return send(bks.at[:, mine(p), :], bkr.at[slot], s3.at[p], r3.at[slot], p)

    loop(1, N, lambda i: back_copy(lax.rem(t + i, N), t).start())
    bkr[t] = bks[:, mine(t), :]
    stage_x2(3)
    for p in range(4):
        stage_x3(p)

    def wait_back(i):
        p = lax.rem(t + i, N)
        back_copy(p, p).wait_recv()

    loop(1, N, wait_back)
    jn = lanes & 31

    for n in reversed(range(SEC)):

        def backward(pr, n=n):
            t0, t1 = pair_of(n, pr)
            grads = jnp.zeros((SUB, TOK), F32)
            lows, highs = [], []
            for j in range(4):
                cs, sn = ccos[n, pr, j], csin[n, pr, j]
                gl, gu = bkr[t0, j].astype(F32), bkr[t1, j].astype(F32)
                low = cs * gl + sn * gu
                high = cs * gu - sn * gl
                e = state(n, t0, j) * high - state(n, t1, j) * low
                total = jnp.sum(e, axis=1, keepdims=True) * (1.0 + cs)
                grads = jnp.where(jn == j * SEC + n, total, grads)
                lows.append(low)
                highs.append(high)
                if n:
                    bkr[t0, j] = low.astype(BF16)
                    bkr[t1, j] = high.astype(BF16)
            if n == 0:
                for blk, parts in ((t0, lows), (t1, highs)):
                    gs[blk, 0] = (parts[0] + parts[1] + parts[2]).astype(BF16)
                    gs[blk, 1] = parts[3].astype(BF16)
            for blk in (t0, t1):
                whole = grads if n == SEC - 1 else angbuf[blk] + grads
                if n:
                    angbuf[blk] = whole
                else:
                    top = whole.astype(BF16).astype(F32)
                    gs[blk, 2] = jnp.where(lanes < 32, top, whole - top).astype(BF16)

        loop(0, 16, backward)

    def out_copy(p, src):
        return send(gs.at[p], gt.at[:, mine(src), :], s4.at[p], r4.at[src], p)

    loop(1, N, lambda i: out_copy(lax.rem(t + i, N), t).start())
    gt[:, mine(t), :] = gs[t]

    for p in range(3):
        src = lax.rem(z + 1 + p, 4)
        z_copy(0, src).wait_recv()
    total = accx[z].astype(F32)
    for p in range(3):
        total = total + rz[lax.rem(z + 1 + p, 4)].astype(F32)
    total = total.astype(BF16)
    q_out[:, 0:128] = total[0:128]
    q_out[:, 128:256] = total[128:256]
    o_out[:, 0:128] = total[256:384]
    o_out[:, 128:256] = total[384:512]
    k_out[...] = dot_nt(eye(TOK), total[512:544]).astype(BF16)
    v_out[...] = dot_nt(eye(TOK), total[544:576]).astype(BF16)

    def wait_out(i):
        p = lax.rem(t + i, N)
        out_copy(p, p).wait_recv()

    loop(1, N, wait_out)

    def natural(k):
        turned = dot_nt(eye(TOK), gt[k]).astype(BF16)
        return dot(turned, perm[...])

    both = natural(2)
    angd[d] = both[0:32] + both[32:64]

    def ang_copy(p, slot):
        return send(angd.at[slot], angd.at[slot], sd.at[p], rd.at[slot], p, "dp")

    loop(1, DP, lambda i: ang_copy(lax.rem(d + i, DP), d).start())
    tg[...] = natural(0).astype(BF16)
    mg[...] = natural(1).astype(BF16)

    def wait_ang(i):
        p = lax.rem(d + i, DP)
        ang_copy(p, p).wait_recv()

    loop(1, DP, wait_ang)
    grads = angd[0]
    for i in range(1, DP):
        grads = grads + angd[i]
    for j in range(4):
        ang_out[j] = grads[j * SEC : j * SEC + SEC]

    def drain(i):
        p = lax.rem(t + i, N)
        in_copy(p, t).wait_send()
        h5_copy(p, t).wait_send()
        back_copy(p, t).wait_send()
        out_copy(p, t).wait_send()

    loop(1, N, drain)
    loop(0, 31, lambda i: ag_copy(i, x, z, sib, ag_r).wait_send())
    for p in range(4):
        a_copy(p).wait_send()
        for way in range(2):
            x1_copy(p, way).wait_send()
            x2_copy(p, way).wait_send()
        if p < 3:
            z_copy(p, z).wait_send()
    loop(1, DP, lambda i: ang_copy(lax.rem(d + i, DP), d).wait_send())


def shards(*args):
    def vm(shape, dtype=BF16):
        return pltpu.VMEM(shape, dtype)

    def sem(n):
        return pltpu.SemaphoreType.DMA((n,))

    scratch = [
        vm((128, 8192), F32), vm((128, 1024), F32), vm((128, 1024), F32), vm((128, 8192), F32),
        vm((CH, 8192)), vm((CH, 1024)), vm((CH, 1024)), vm((CH, 8192)),
        vm((CH, CH)),
        vm((2, CH, TOK)), vm((N, 2, SUB, TOK)),
        vm((SEC - 1, N, 4, SUB, TOK)), vm((N, 4, SUB, TOK)),
        vm((4, CH, TOK)), vm((4, TOK, CH)),
        vm((SEC, 16, 4, SUB, TOK), F32), vm((SEC, 16, 4, SUB, TOK), F32),
        vm((N, ROWS, TOK)), vm((N, ROWS, TOK)),
        vm((16, ROWS, TOK)),
        vm((4, 2, HALF, TOK)), vm((4, 2, ROWS, TOK)),
        vm((4, ROWS, TOK)), vm((4, ROWS, TOK)),
        vm((CH, TOK), F32), vm((1024, TOK)),
        vm((4, CH, TOK)), vm((N, 4, SUB, TOK)),
        vm((N, 3, SUB, TOK)), vm((3, CH, TOK)),
        vm((N, SUB, TOK), F32), vm((DP, 32, CH), F32),
        sem(4), sem(N), sem(N), sem(N), sem(N), sem(N), sem(N), sem(N), sem(N),
        sem(31), sem(16), sem(16), sem(4), sem(4), sem(8), sem(8), sem(8), sem(8),
        sem(4), sem(4), sem(DP), sem(DP),
    ]
    outs = [
        jax.ShapeDtypeStruct((TOK, 256), BF16),
        jax.ShapeDtypeStruct((TOK, 32), BF16),
        jax.ShapeDtypeStruct((TOK, 32), BF16),
        jax.ShapeDtypeStruct((TOK, 256), BF16),
        jax.ShapeDtypeStruct((TOK, CH), BF16),
        jax.ShapeDtypeStruct((TOK, CH), BF16),
        jax.ShapeDtypeStruct((4, SEC, CH), F32),
    ]
    in_vmem = pl.BlockSpec(memory_space=pltpu.VMEM)
    in_any = pl.BlockSpec(memory_space=pl.ANY)
    return pl.pallas_call(
        kernel,
        out_shape=outs,
        in_specs=[in_any if i in (3, 5, 7, 9) else in_vmem for i in range(15)],
        out_specs=[in_vmem] * 7,
        scratch_shapes=scratch,
        compiler_params=pltpu.CompilerParams(
            collective_id=0, has_side_effects=True, vmem_limit_bytes=62 * 1024 * 1024
        ),
        cost_estimate=pl.CostEstimate(
            flops=4 * TOK * CH * 18432, bytes_accessed=12_000_000, transcendentals=0
        ),
    )(*args)


def solution(mesh):
    both = P("dp", "tensor")
    rows = P("tensor", None)
    return jax.shard_map(
        shards,
        mesh=mesh,
        in_specs=(both, both, P(), rows, rows, rows, rows, rows, rows, rows, rows)
        + (both, both, both, both),
        out_specs=(both, both, both, both, both, both, P(None, None, "tensor")),
        check_vma=False,
    )
```

```python
import jax
import jax.numpy as jnp
from jax import lax
from jax.experimental import pallas as pl
from jax.experimental.pallas import tpu as pltpu
from jax.sharding import PartitionSpec as P

F32 = jnp.float32
BF16 = jnp.bfloat16
MESH = pl.DeviceIdType.MESH
N = 32
BU = 2
CH = 512
SUB = 16
TOK = 128
SEC = 5
ROWS = 576
HALF = 288
NT = (((1,), (1,)), ((), ()))


def dot(a, b):
    return jnp.dot(a, b, preferred_element_type=F32)


def dot_nt(a, b):
    return lax.dot_general(a, b, NT, preferred_element_type=F32)


def eye(n):
    r = lax.broadcasted_iota(jnp.int32, (n, n), 0)
    c = lax.broadcasted_iota(jnp.int32, (n, n), 1)
    return jnp.where(r == c, 1.0, 0.0).astype(BF16)


def loop(lo, hi, fn, unroll=1):
    def step(i, carry):
        fn(i)
        return carry

    lax.fori_loop(lo, hi, step, 0, unroll=unroll)


def dequantize(packed, scale, out, first, width):
    def chunk(i):
        cols = pl.ds(pl.multiple_of(first + i * 128, 128), 128)
        spread = scale[:, cols].astype(F32)
        for g in range(8):
            rows = slice(16 * g, 16 * g + 16)
            word = packed[rows, cols].astype(jnp.int32)
            s = jnp.broadcast_to(spread[g : g + 1, :], (16, 128))
            for plane in range(4):
                digit = (word >> (4 * plane)) & 15 if plane < 3 else word >> 12
                value = (digit.astype(F32) - 7.5) * s
                out[128 * plane + 16 * g : 128 * plane + 16 * g + 16, cols] = value.astype(BF16)

    loop(0, width // 128, chunk)


def add_rows(dst, base, rows, srcs, out=None, out_base=0):
    def step(i):
        off = pl.multiple_of(i * 96, 96)
        total = dst[base, pl.ds(rows[0] + off, 96), :].astype(F32)
        for ref, index, first in srcs:
            total = total + ref[index + (pl.ds(first + off, 96), slice(None))].astype(F32)
        if out is None:
            dst[base, pl.ds(rows[0] + off, 96), :] = total.astype(BF16)
        else:
            out[out_base, pl.ds(rows[0] + off, 96), :] = total.astype(BF16)

    loop(0, (rows[1] - rows[0]) // 96, step)


def kernel(
    tok, mix, ang, qp, qs, kp, ks, vp, vs, op, os_, qc, kc, vc, oc,
    q_out, k_out, v_out, o_out, tg, mg, ang_out,
    packq, packk, packv, packo, wq, wk, wv, wo, perm,
    tok_t, hin, st, h5s, h5t, hl, ccos, csin,
    ag, part, ra, rx1, rx2, accx, rz, acc, bks, bkr, gb, gs, gt, angy, angz, spread, angs, angt,
    ld, s1, r1, s2, r2, s3, r3, s4, r4, ag_s, ag_r, ag_sib, ra_s, ra_r, rx1_s, rx1_r,
    rx2_s, rx2_r, rz_s, rz_r, sd, rd, s5, r5,
):
    d = lax.axis_index("dp")
    t = lax.axis_index("tensor")
    x = lax.div(t, 8)
    z = lax.rem(lax.div(t, 2), 4)
    c = lax.rem(t, 2)
    xp, xm, x2 = lax.rem(x + 1, 4), lax.rem(x + 3, 4), lax.rem(x + 2, 4)

    def dev(x_, z_, c_):
        return (x_ * 4 + z_) * 2 + c_

    sib = dev(x, z, 1 - c)
    y, zh = lax.div(d, 2), lax.rem(d, 2)
    far = y * 2 + 1 - zh
    dp_peers = [lax.rem(y + i, 4) * 2 + zh for i in (1, 2, 3)] + [far]

    def send(src, dst, ssem, rsem, peer, axis="tensor"):
        return pltpu.make_async_remote_copy(
            src_ref=src, dst_ref=dst, send_sem=ssem, recv_sem=rsem,
            device_id={axis: peer}, device_id_type=MESH,
        )

    loads = [
        pltpu.make_async_copy(src, dst, ld.at[i])
        for i, (src, dst) in enumerate(((kp, packk), (vp, packv), (qp, packq), (op, packo)))
    ]
    for load in loads:
        load.start()
    bar = pltpu.get_barrier_semaphore()
    loop(1, N, lambda i: pl.semaphore_signal(
        bar, inc=1, device_id={"tensor": lax.rem(t + i, N)}, device_id_type=MESH))
    for peer in dp_peers:
        pl.semaphore_signal(bar, inc=1, device_id={"dp": peer}, device_id_type=MESH)

    r = lax.broadcasted_iota(jnp.int32, (CH, CH), 0)
    col = lax.broadcasted_iota(jnp.int32, (CH, CH), 1)
    perm[...] = jnp.where(col == 4 * (r & 127) + (r >> 7), 1.0, 0.0).astype(BF16)
    tok_t[0] = dot_nt(perm[...], tok[...]).astype(BF16)
    tok_t[1] = dot_nt(perm[...], mix[...]).astype(BF16)
    own = c * 16 + x * 4 + z
    ag[own, 0:256, :] = dot_nt(eye(256), qc[...]).astype(BF16)
    ag[own, 256:512, :] = dot_nt(eye(256), oc[...]).astype(BF16)
    ag[own, 512:544, :] = kc[...]
    ag[own, 544:576, :] = vc[...]
    pl.semaphore_wait(bar, N - 1 + 4)

    def mine(p):
        return pl.ds(pl.multiple_of(p * SUB, SUB), SUB)

    def in_copy(p, slot):
        return send(tok_t.at[:, mine(p), :], hin.at[slot], s1.at[p], r1.at[slot], p)

    loop(1, N, lambda i: in_copy(lax.rem(t + i, N), t).start())
    hin[t] = tok_t[:, mine(t), :]

    def ag_copy(k, x_, z_, peer, sems):
        slot = c * 16 + x_ * 4 + z_
        return send(ag.at[slot], ag.at[slot], ag_s.at[k], sems.at[x_ * 4 + z_], peer)

    def ag_wait(x_, z_, sems):
        slot = c * 16 + x_ * 4 + z_
        send(ag.at[slot], ag.at[slot], ag_s.at[0], sems.at[x_ * 4 + z_], sib).wait_recv()

    def zrel(dz):
        return lax.rem(z + dz, 4)

    for dz in (1, 2, 3):
        ag_copy(dz - 1, x, z, dev(x, zrel(dz), c), ag_r).start()

    def ag_row(dz):
        ag_copy(3 + 2 * dz, x, zrel(dz), dev(xp, z, c), ag_r).start()
        ag_copy(4 + 2 * dz, x, zrel(dz), dev(xm, z, c), ag_r).start()
        ag_copy(15 + dz, x, zrel(dz), sib, ag_sib).start()

    ag_row(0)

    lanes = lax.broadcasted_iota(jnp.int32, (SUB, TOK), 1)
    subs = lax.broadcasted_iota(jnp.int32, (SUB, TOK), 0)
    pick = lanes == 4 * subs + (64 * c + x)
    window = 128 * lax.div(lax.rem(t, 8), 2)

    def factors(pr):
        where = pl.ds(pl.multiple_of(pr * CH + window, 128), 128)
        for j in range(4):
            for n in range(SEC):
                row = jnp.broadcast_to(ang[n, j : j + 1, where], (SUB, TOK))
                angle = jnp.sum(jnp.where(pick, row, 0.0), axis=1, keepdims=True)
                square = angle * angle
                inverse = 1.0 / (1.0 + square)
                ccos[n, pr, j] = jnp.broadcast_to((1.0 - square) * inverse, (SUB, TOK))
                csin[n, pr, j] = jnp.broadcast_to(2.0 * angle * inverse, (SUB, TOK))

    loop(0, 16, factors)
    loads[0].wait()
    dequantize(packk, ks, wk, 0, 1024)
    loads[1].wait()
    dequantize(packv, vs, wv, 0, 1024)

    def wait_in(i):
        p = lax.rem(t + i, N)
        in_copy(p, p).wait_recv()

    loop(1, N, wait_in)

    def pair_of(n, pr):
        sh = 4 - n
        low = ((pr >> sh) << (sh + 1)) + (pr & ((1 << sh) - 1))
        return low, low + (1 << sh)

    def state(n, blk, j):
        if n == 0:
            return hin[blk, 0 if j < 3 else 1].astype(F32)
        return st[n - 1, blk, j].astype(F32)

    for n in range(SEC):

        def forward(pr, n=n):
            t0, t1 = pair_of(n, pr)
            for j in range(4):
                a, b = state(n, t0, j), state(n, t1, j)
                cs, sn = ccos[n, pr, j], csin[n, pr, j]
                low = (cs * a - sn * b).astype(BF16)
                high = (sn * a + cs * b).astype(BF16)
                if n < SEC - 1:
                    st[n, t0, j] = low
                    st[n, t1, j] = high
                else:
                    h5s[t0, j] = low
                    h5s[t1, j] = high

        loop(0, 16, forward)

    def h5_copy(p, src):
        return send(h5s.at[p], h5t.at[:, mine(src), :], s2.at[p], r2.at[src], p)

    loop(1, N, lambda i: h5_copy(lax.rem(t + i, N), t).start())
    h5t[:, mine(t), :] = h5s[t]

    for dz in (1, 3, 2):
        ag_wait(x, zrel(dz), ag_r)
        ag_row(dz)
    loads[2].wait()
    for dz in range(4):
        dequantize(packq, qs, wq, 2048 * dz, 2048)
        ag_wait(xm, zrel(dz), ag_r)
        if dz % 2 == 0:
            ag_copy(11 + dz // 2, xm, zrel(dz), dev(xp, z, c), ag_r).start()
        ag_copy(19 + dz, xm, zrel(dz), sib, ag_sib).start()
        ag_wait(xp, zrel(dz), ag_r)
        if dz % 2 == 1:
            ag_copy(13 + dz // 2, xp, zrel(dz), dev(xm, z, c), ag_r).start()
        ag_copy(23 + dz, xp, zrel(dz), sib, ag_sib).start()
    loads[3].wait()
    for dz in range(4):
        dequantize(packo, os_, wo, 2048 * dz, 2048)
        ag_wait(x2, zrel(dz), ag_r)
        ag_copy(27 + dz, x2, zrel(dz), sib, ag_sib).start()

    def wait_h5(i):
        p = lax.rem(t + i, N)
        h5_copy(p, p).wait_recv()

    def narrow(j, w, first):
        piece = dot(hl[j], w[...]).astype(BF16)
        for i in range(8):
            turned = dot_nt(eye(TOK), piece[:, 128 * i : 128 * i + 128]).astype(BF16)
            for k in range(4):
                slot = ((k % 2) * 4 + 2 * (i % 2) + k // 2) * 4 + i // 2
                part[slot, first : first + 32, :] = turned[32 * k : 32 * k + 32, :]

    def wide(zp):
        def column(x_):
            cols = pl.ds(pl.multiple_of((x_ * 4 + zp) * 512, 512), 512)
            for j, w, first in ((0, wq, 0), (3, wo, 256)):
                piece = dot(hl[j], w[:, cols]).astype(BF16)
                for c_ in range(2):
                    for half in range(2):
                        at = c_ * 256 + half * 128
                        rows = slice(first + half * 128, first + half * 128 + 128)
                        part[(c_ * 4 + zp) * 4 + x_, rows, :] = piece[:, at : at + 128]

        loop(0, 4, column)

    def piece_z(p):
        return lax.rem(z + 1 + p, 4)

    def base(zp):
        return (c * 4 + zp) * 4

    def a_copy(p):
        zp = piece_z(p)
        return send(
            part.at[pl.ds(((1 - c) * 4 + zp) * 4, 4)], ra.at[pl.ds(zp * 4, 4)],
            ra_s.at[p], ra_r.at[p], sib,
        )

    def x1_copy(p, way):
        zp = piece_z(p)
        return send(
            part.at[base(zp) + x2, pl.ds(way * HALF, HALF), :], rx1.at[zp, way],
            rx1_s.at[2 * p + way], rx1_r.at[2 * p + way], dev(xm if way else xp, z, c),
        )

    def x2_copy(p, way):
        zp = piece_z(p)
        to = xm if way else xp
        return send(
            part.at[base(zp) + to], rx2.at[zp, way],
            rx2_s.at[2 * p + way], rx2_r.at[2 * p + way], dev(to, z, c),
        )

    def z_copy(p, src):
        zp = piece_z(p)
        return send(accx.at[zp], rz.at[src], rz_s.at[p], rz_r.at[src], dev(x, zp, c))

    def stage_x1(p):
        zp = piece_z(p)
        a_copy(p).wait_recv()
        add_rows(part, base(zp) + x2, (0, ROWS), [(ra, (zp * 4 + x2,), 0)])
        x1_copy(p, 0).start()
        x1_copy(p, 1).start()
        for x_ in (xp, xm, x):
            add_rows(part, base(zp) + x_, (0, ROWS), [(ra, (zp * 4 + x_,), 0)])

    def stage_x2(p):
        zp = piece_z(p)
        x1_copy(p, 0).wait_recv()
        add_rows(part, base(zp) + xp, (0, HALF), [(rx1, (zp, 0), 0)])
        x2_copy(p, 0).start()
        x1_copy(p, 1).wait_recv()
        add_rows(part, base(zp) + xm, (HALF, ROWS), [(rx1, (zp, 1), 0)])
        x2_copy(p, 1).start()

    def stage_x3(p):
        zp = piece_z(p)
        x2_copy(p, 0).wait_recv()
        x2_copy(p, 1).wait_recv()
        add_rows(part, base(zp) + x, (0, ROWS), [(rx2, (zp, 0), 0), (rx2, (zp, 1), 0)], accx, zp)
        if p < 3:
            z_copy(p, z).start()

    for x_ in range(4):
        for z_ in range(4):
            slot = (1 - c) * 16 + x_ * 4 + z_
            send(
                ag.at[slot], ag.at[slot], ag_s.at[0], ag_sib.at[x_ * 4 + z_], sib
            ).wait_recv()

    def back_wide(j, w, first):
        total = None
        for quarter in range(4):
            rhs = jnp.concatenate(
                [
                    ag[c_ * 16 + 4 * quarter + i, first : first + 256, :]
                    for i in range(4)
                    for c_ in range(2)
                ],
                axis=0,
            )
            piece = dot(w[:, 2048 * quarter : 2048 * quarter + 2048], rhs)
            if quarter == 0:
                acc[...] = piece
            elif quarter < 3:
                acc[...] += piece
            else:
                bks[j] = (acc[...] + piece).astype(BF16)

    def back_narrow(j, w, first):
        rhs = jnp.concatenate(
            [ag[c_ * 16 + i, first : first + 32, :] for i in range(16) for c_ in range(2)], axis=0
        )
        bks[j] = dot(w[...], rhs).astype(BF16)

    def back_copy(k, p, slot):
        js = pl.ds(0, 3) if k == 0 else pl.ds(3, 1)
        return send(
            bks.at[js, mine(p), :], bkr.at[slot, js], s3.at[k * N + p], r3.at[k * N + slot], p
        )

    back_wide(0, wq, 0)
    back_narrow(1, wk, 512)
    back_narrow(2, wv, 544)
    loop(1, N, lambda i: back_copy(0, lax.rem(t + i, N), t).start())
    back_wide(3, wo, 256)
    loop(1, N, lambda i: back_copy(1, lax.rem(t + i, N), t).start())
    bkr[t] = bks[:, mine(t), :]

    loop(1, N, wait_h5)
    for j in range(4):
        hl[j] = dot_nt(eye(TOK), h5t[j]).astype(BF16)
    narrow(1, wk, 512)
    narrow(2, wv, 544)
    for p in range(4):
        wide(piece_z(p))
        a_copy(p).start()
        if p:
            stage_x1(p - 1)
    stage_x1(3)
    stage_x2(0)
    stage_x2(1)
    stage_x3(0)

    def wait_back(i):
        p = lax.rem(t + i, N)
        back_copy(0, p, p).wait_recv()
        back_copy(1, p, p).wait_recv()

    loop(1, N, wait_back)

    for n in reversed(range(SEC)):
        take, put = (bkr, gb) if n % 2 == 0 else (gb, bkr)

        def backward(pr, grads, n=n, take=take, put=put):
            t0, t1 = pair_of(n, pr)
            lows, highs = [], []
            for j in range(4):
                cs, sn = ccos[n, pr, j], csin[n, pr, j]
                gl, gu = take[t0, j].astype(F32), take[t1, j].astype(F32)
                low = cs * gl + sn * gu
                high = cs * gu - sn * gl
                e = state(n, t0, j) * high - state(n, t1, j) * low
                total = jnp.sum(e, axis=1, keepdims=True) * (1.0 + cs)
                grads = jnp.where(lanes == pr * 4 + j, total, grads)
                lows.append(low)
                highs.append(high)
                if n:
                    put[t0, j] = low.astype(BF16)
                    put[t1, j] = high.astype(BF16)
            if n == 0:
                for blk, parts in ((t0, lows), (t1, highs)):
                    gs[blk, 0] = (parts[0] + parts[1] + parts[2]).astype(BF16)
                    gs[blk, 1] = parts[3].astype(BF16)
            return grads

        angy[y, n] = lax.fori_loop(0, 16, backward, jnp.zeros((SUB, TOK), F32), unroll=BU)
        if n == 4:
            stage_x2(2)
        elif n == 3:
            stage_x3(1)
        elif n == 2:
            stage_x2(3)
        elif n == 1:
            stage_x3(2)

    def y_copy(k, slot):
        return send(angy.at[slot], angy.at[slot], sd.at[k], rd.at[slot], dp_peers[k], "dp")

    for k in range(3):
        y_copy(k, y).start()

    def out_copy(p, src):
        return send(gs.at[p], gt.at[:, mine(src), :], s4.at[p], r4.at[src], p)

    loop(1, N, lambda i: out_copy(lax.rem(t + i, N), t).start())
    gt[:, mine(t), :] = gs[t]
    stage_x3(3)
    for k in range(3):
        y_copy(k, lax.rem(y + 1 + k, 4)).wait_recv()
    for n in range(SEC):
        angz[zh, n] = ((angy[0, n] + angy[1, n]) + angy[2, n]) + angy[3, n]

    def far_copy(slot):
        return send(angz.at[slot], angz.at[slot], sd.at[3], rd.at[4], far, "dp")

    far_copy(zh).start()

    for p in range(3):
        src = lax.rem(z + 1 + p, 4)
        z_copy(0, src).wait_recv()
    total = accx[z].astype(F32)
    for p in range(3):
        total = total + rz[lax.rem(z + 1 + p, 4)].astype(F32)
    total = total.astype(BF16)
    q_out[:, 0:128] = total[0:128]
    q_out[:, 128:256] = total[128:256]
    o_out[:, 0:128] = total[256:384]
    o_out[:, 128:256] = total[384:512]
    k_out[...] = total[512:544]
    v_out[...] = total[544:576]

    far_copy(1 - zh).wait_recv()
    for n in range(SEC):
        whole = angz[0, n] + angz[1, n]
        for pr in range(16):
            moved = pltpu.roll(whole, (4 * n - 4 * pr) % TOK, 1)
            keep = (lanes >= 4 * n) & (lanes < 4 * n + 4)
            spread[n, pr] = jnp.where(keep, moved, 0.0)

    def message(blk):
        whole = jnp.zeros((SUB, TOK), F32)
        for n in range(SEC):
            sh = 4 - n
            whole = whole + spread[n, ((blk >> (sh + 1)) << sh) + (blk & ((1 << sh) - 1))]
        top = whole.astype(BF16).astype(F32)
        rest = pltpu.roll(whole - top, 32, 1)
        angs[blk] = jnp.where(lanes < 32, top, rest).astype(BF16)

    def ang_copy(p, src):
        return send(angs.at[p], angt.at[mine(src), :], s5.at[p], r5.at[src], p)

    loop(0, N, message, unroll=4)
    loop(1, N, lambda i: ang_copy(lax.rem(t + i, N), t).start())
    angt[mine(t), :] = angs[t]

    def wait_out(i):
        p = lax.rem(t + i, N)
        out_copy(p, p).wait_recv()

    loop(1, N, wait_out)

    def natural(value):
        return dot(dot_nt(eye(TOK), value).astype(BF16), perm[...])

    tg[...] = natural(gt[0]).astype(BF16)
    mg[...] = natural(gt[1]).astype(BF16)

    def wait_ang(i):
        p = lax.rem(t + i, N)
        ang_copy(p, p).wait_recv()

    loop(1, N, wait_ang)
    both = natural(angt[...])
    ang_out[...] = both[0:32] + both[32:64]

    def drain(i):
        p = lax.rem(t + i, N)
        in_copy(p, t).wait_send()
        h5_copy(p, t).wait_send()
        back_copy(0, p, t).wait_send()
        back_copy(1, p, t).wait_send()
        ang_copy(p, t).wait_send()
        out_copy(p, t).wait_send()

    loop(1, N, drain)
    loop(0, 31, lambda i: ag_copy(i, x, z, sib, ag_r).wait_send())
    for p in range(4):
        a_copy(p).wait_send()
        for way in range(2):
            x1_copy(p, way).wait_send()
            x2_copy(p, way).wait_send()
        if p < 3:
            z_copy(p, z).wait_send()
    for k in range(3):
        y_copy(k, y).wait_send()
    far_copy(zh).wait_send()


def shards(*args):
    def vm(shape, dtype=BF16):
        return pltpu.VMEM(shape, dtype)

    def sem(n):
        return pltpu.SemaphoreType.DMA((n,))

    scratch = [
        vm((128, 8192), F32), vm((128, 1024), F32), vm((128, 1024), F32), vm((128, 8192), F32),
        vm((CH, 8192)), vm((CH, 1024)), vm((CH, 1024)), vm((CH, 8192)),
        vm((CH, CH)),
        vm((2, CH, TOK)), vm((N, 2, SUB, TOK)),
        vm((SEC - 1, N, 4, SUB, TOK)), vm((N, 4, SUB, TOK)),
        vm((4, CH, TOK)), vm((4, TOK, CH)),
        vm((SEC, 16, 4, SUB, TOK), F32), vm((SEC, 16, 4, SUB, TOK), F32),
        vm((N, ROWS, TOK)), vm((N, ROWS, TOK)),
        vm((16, ROWS, TOK)),
        vm((4, 2, HALF, TOK)), vm((4, 2, ROWS, TOK)),
        vm((4, ROWS, TOK)), vm((4, ROWS, TOK)),
        vm((CH, TOK), F32),
        vm((4, CH, TOK)), vm((N, 4, SUB, TOK)), vm((N, 4, SUB, TOK)),
        vm((N, 2, SUB, TOK)), vm((2, CH, TOK)),
        vm((4, SEC, SUB, TOK), F32), vm((2, SEC, SUB, TOK), F32),
        vm((SEC, 16, SUB, TOK), F32), vm((N, SUB, TOK)), vm((CH, TOK)),
        sem(4), sem(N), sem(N), sem(N), sem(N), sem(2 * N), sem(2 * N), sem(N), sem(N),
        sem(31), sem(16), sem(16), sem(4), sem(4), sem(8), sem(8), sem(8), sem(8),
        sem(4), sem(4), sem(4), sem(5), sem(N), sem(N),
    ]
    shapes = [(TOK, 256), (32, TOK), (32, TOK), (TOK, 256), (TOK, CH), (TOK, CH)]
    outs = [jax.ShapeDtypeStruct(shape, BF16) for shape in shapes]
    in_vmem = pl.BlockSpec(memory_space=pltpu.VMEM)
    in_any = pl.BlockSpec(memory_space=pl.ANY)
    args = list(args)
    args[2] = args[2].transpose(1, 0, 2)
    args[12], args[13] = args[12].T, args[13].T
    results = pl.pallas_call(
        kernel,
        out_shape=outs + [jax.ShapeDtypeStruct((32, CH), F32)],
        in_specs=[in_any if i in (3, 5, 7, 9) else in_vmem for i in range(15)],
        out_specs=[in_vmem] * 7,
        scratch_shapes=scratch,
        compiler_params=pltpu.CompilerParams(
            collective_id=0, has_side_effects=True, vmem_limit_bytes=62 * 1024 * 1024
        ),
        cost_estimate=pl.CostEstimate(
            flops=4 * TOK * CH * 18432, bytes_accessed=12_000_000, transcendentals=0
        ),
    )(*args)

    def hand_over(*refs):
        for src, dst in zip(refs[:6], refs[7:13]):
            dst[...] = src[...]
        for n in range(SEC):
            refs[13][n] = refs[6][4 * n : 4 * n + 4, :]

    final = pl.pallas_call(
        hand_over,
        out_shape=outs + [jax.ShapeDtypeStruct((SEC, 4, CH), F32)],
        in_specs=[in_vmem] * 7,
        out_specs=[in_vmem] * 7,
    )(*results)
    q_out, k_out, v_out, o_out, tg, mg, ang = final
    return q_out, k_out.T, v_out.T, o_out, tg, mg, ang.transpose(1, 0, 2)


def solution(mesh):
    both = P("dp", "tensor")
    rows = P("tensor", None)
    return jax.shard_map(
        shards,
        mesh=mesh,
        in_specs=(both, both, P(), rows, rows, rows, rows, rows, rows, rows, rows)
        + (both, both, both, both),
        out_specs=(both, both, both, both, both, both, P(None, None, "tensor")),
        check_vma=False,
    )
```

```python
import jax
import jax.numpy as jnp
from jax import lax
from jax.experimental import pallas as pl
from jax.experimental.pallas import tpu as pltpu
from jax.sharding import PartitionSpec as P

F32 = jnp.float32
BF16 = jnp.bfloat16
MESH = pl.DeviceIdType.MESH
N = 32
BU = 2
CH = 512
SUB = 16
TOK = 128
SEC = 5
ROWS = 576
HALF = 288
PARTS = (pl.ds(0, 320), pl.ds(320, 256))
NT = (((1,), (1,)), ((), ()))


def dot(a, b):
    return jnp.dot(a, b, preferred_element_type=F32)


def dot_nt(a, b):
    return lax.dot_general(a, b, NT, preferred_element_type=F32)


def eye(n):
    r = lax.broadcasted_iota(jnp.int32, (n, n), 0)
    c = lax.broadcasted_iota(jnp.int32, (n, n), 1)
    return jnp.where(r == c, 1.0, 0.0).astype(BF16)


def loop(lo, hi, fn, unroll=1):
    def step(i, carry):
        fn(i)
        return carry

    lax.fori_loop(lo, hi, step, 0, unroll=unroll)


def dequantize(packed, scale, out, first, width):
    def chunk(i):
        cols = pl.ds(pl.multiple_of(first + i * 128, 128), 128)
        spread = scale[:, cols].astype(F32)
        for g in range(8):
            rows = slice(16 * g, 16 * g + 16)
            word = packed[rows, cols].astype(jnp.int32)
            s = jnp.broadcast_to(spread[g : g + 1, :], (16, 128))
            for plane in range(4):
                digit = (word >> (4 * plane)) & 15 if plane < 3 else word >> 12
                value = (digit.astype(F32) - 7.5) * s
                out[128 * plane + 16 * g : 128 * plane + 16 * g + 16, cols] = value.astype(BF16)

    loop(0, width // 128, chunk)


def add_rows(dst, base, rows, srcs, out=None, out_base=0):
    def step(i):
        off = pl.multiple_of(i * 96, 96)
        total = dst[base, pl.ds(rows[0] + off, 96), :].astype(F32)
        for ref, index, first in srcs:
            total = total + ref[index + (pl.ds(first + off, 96), slice(None))].astype(F32)
        if out is None:
            dst[base, pl.ds(rows[0] + off, 96), :] = total.astype(BF16)
        else:
            out[out_base, pl.ds(rows[0] + off, 96), :] = total.astype(BF16)

    loop(0, (rows[1] - rows[0]) // 96, step)


def kernel(
    tok, mix, ang, qp, qs, kp, ks, vp, vs, op, os_, qc, kc, vc, oc,
    q_out, k_out, v_out, o_out, tg, mg, ang_out,
    packq, packk, packv, packo, wq, wk, wv, wo, perm,
    tok_t, hin, st, h5s, h5t, hl, ccos, csin,
    ag, part, ra, rx1, rx2, accx, rz, acc, bks, bkr, gb, gs, gt, angy, angz, spread, angs, angt,
    ld, s1, r1, s2, r2, s3, r3, s4, r4, ag_s, ag_r, ag_sib, ra_s, ra_r, rx1_s, rx1_r,
    rx2_s, rx2_r, rz_s, rz_r, sd, rd, s5, r5,
):
    d = lax.axis_index("dp")
    t = lax.axis_index("tensor")
    x = lax.div(t, 8)
    z = lax.rem(lax.div(t, 2), 4)
    c = lax.rem(t, 2)
    xp, xm, x2 = lax.rem(x + 1, 4), lax.rem(x + 3, 4), lax.rem(x + 2, 4)

    def dev(x_, z_, c_):
        return (x_ * 4 + z_) * 2 + c_

    sib = dev(x, z, 1 - c)
    y, zh = lax.div(d, 2), lax.rem(d, 2)
    far = y * 2 + 1 - zh
    dp_peers = [lax.rem(y + i, 4) * 2 + zh for i in (1, 2, 3)] + [far]

    def send(src, dst, ssem, rsem, peer, axis="tensor"):
        return pltpu.make_async_remote_copy(
            src_ref=src, dst_ref=dst, send_sem=ssem, recv_sem=rsem,
            device_id={axis: peer}, device_id_type=MESH,
        )

    bar = pltpu.get_barrier_semaphore()
    loop(1, N, lambda i: pl.semaphore_signal(
        bar, inc=1, device_id={"tensor": lax.rem(t + i, N)}, device_id_type=MESH))
    for peer in dp_peers:
        pl.semaphore_signal(bar, inc=1, device_id={"dp": peer}, device_id_type=MESH)

    loads = [
        pltpu.make_async_copy(src, dst, ld.at[i])
        for i, (src, dst) in enumerate(((kp, packk), (vp, packv), (qp, packq), (op, packo)))
    ]
    for load in loads:
        load.start()
    r = lax.broadcasted_iota(jnp.int32, (CH, CH), 0)
    col = lax.broadcasted_iota(jnp.int32, (CH, CH), 1)
    perm[...] = jnp.where(col == 4 * (r & 127) + (r >> 7), 1.0, 0.0).astype(BF16)
    tok_t[0] = dot_nt(perm[...], tok[...]).astype(BF16)
    tok_t[1] = dot_nt(perm[...], mix[...]).astype(BF16)
    own = c * 16 + x * 4 + z
    ag[own, 0:256, :] = dot_nt(eye(256), qc[...]).astype(BF16)
    ag[own, 320:576, :] = dot_nt(eye(256), oc[...]).astype(BF16)
    ag[own, 256:288, :] = kc[...]
    ag[own, 288:320, :] = vc[...]
    lanes = lax.broadcasted_iota(jnp.int32, (SUB, TOK), 1)
    subs = lax.broadcasted_iota(jnp.int32, (SUB, TOK), 0)
    pick = lanes == 4 * subs + (64 * c + x)
    window = 128 * lax.div(lax.rem(t, 8), 2)

    def factors(pr):
        where = pl.ds(pl.multiple_of(pr * CH + window, 128), 128)
        for j in range(4):
            for n in range(SEC):
                row = jnp.broadcast_to(ang[n, j : j + 1, where], (SUB, TOK))
                angle = jnp.sum(jnp.where(pick, row, 0.0), axis=1, keepdims=True)
                square = angle * angle
                inverse = 1.0 / (1.0 + square)
                ccos[n, pr, j] = jnp.broadcast_to((1.0 - square) * inverse, (SUB, TOK))
                csin[n, pr, j] = jnp.broadcast_to(2.0 * angle * inverse, (SUB, TOK))

    loop(0, 16, factors)
    loads[0].wait()
    dequantize(packk, ks, wk, 0, 1024)
    loads[1].wait()
    dequantize(packv, vs, wv, 0, 1024)

    pl.semaphore_wait(bar, N - 1 + 4)

    def mine(p):
        return pl.ds(pl.multiple_of(p * SUB, SUB), SUB)

    def group(ref, ssem, rsem, k=0):
        all_ = ref.at[pl.ds(0, N - 1)]
        return send(all_, all_, ssem.at[k], rsem.at[k], sib)

    def in_copy(p, slot):
        return send(tok_t.at[:, mine(p), :], hin.at[slot], s1.at[0], r1.at[0], p)

    near = z - 1 + 2 * lax.div(3 - z, 3)
    last = 3 * (1 - lax.div(z, 2))
    order = (z, near, 6 - z - near - last, last)

    def ag_copy(k, part_, x_, z_, peer, sems):
        here = ag.at[c * 16 + x_ * 4 + z_, PARTS[part_], :]
        at = part_ * 16 + x_ * 4 + z_
        return send(here, here, ag_s.at[part_ * 33 + k], sems.at[at], peer)

    def ag_wait(part_, x_, z_):
        ag_copy(0, part_, x_, z_, sib, ag_r).wait_recv()

    def upward(part_, k, z_):
        return ag_copy(k, part_, x, z_, dev(x, z + 1, c), ag_r)

    def downward(part_, k, z_):
        return ag_copy(k, part_, x, z_, dev(x, z - 1, c), ag_r)

    def ag_z(part_, act):
        @pl.when(z < 3)
        def _():
            act(upward(part_, 0, z))

        @pl.when(z > 0)
        def _():
            act(downward(part_, 1, z))

    def ag_on(part_, k, act):
        @pl.when((order[k] < z) & (z < 3))
        def _():
            act(upward(part_, 1 + k, order[k]))

        @pl.when((order[k] > z) & (z > 0))
        def _():
            act(downward(part_, 1 + k, order[k]))

    def start(copy):
        copy.start()

    def left(copy):
        copy.wait_send()

    def ag_row(part_, k):
        ag_copy(5 + 2 * k, part_, x, order[k], dev(xp, z, c), ag_r).start()
        ag_copy(6 + 2 * k, part_, x, order[k], dev(xm, z, c), ag_r).start()
        ag_copy(17 + k, part_, x, order[k], sib, ag_sib).start()

    def ag_col(part_, k):
        ag_wait(part_, x, order[k])
        ag_on(part_, k, start)
        ag_row(part_, k)

    def ag_near(part_, k):
        ag_wait(part_, xm, order[k])
        if k % 2 == 0:
            ag_copy(13 + k, part_, xm, order[k], dev(xp, z, c), ag_r).start()
        ag_copy(21 + k, part_, xm, order[k], sib, ag_sib).start()
        ag_wait(part_, xp, order[k])
        if k % 2 == 1:
            ag_copy(13 + k, part_, xp, order[k], dev(xm, z, c), ag_r).start()
        ag_copy(25 + k, part_, xp, order[k], sib, ag_sib).start()

    def ag_far(part_, k):
        ag_wait(part_, x2, order[k])
        ag_copy(29 + k, part_, x2, order[k], sib, ag_sib).start()

    def ag_own(part_):
        for x_ in range(4):
            for z_ in range(4):
                here = ag.at[(1 - c) * 16 + x_ * 4 + z_, PARTS[part_], :]
                at = part_ * 16 + x_ * 4 + z_
                send(here, here, ag_s.at[0], ag_sib.at[at], sib).wait_recv()

    ag_z(0, start)
    ag_row(0, 0)
    loop(1, N, lambda i: in_copy(lax.rem(t + i, N), t).start())
    hin[t] = tok_t[:, mine(t), :]
    ag_z(1, start)
    ag_row(1, 0)

    loads[2].wait()
    dequantize(packq, qs, wq, 0, 2048)
    ag_col(0, 1)
    dequantize(packq, qs, wq, 2048, 2048)
    ag_near(0, 0)
    ag_col(0, 2)

    group(hin, s1, r1).wait_recv()

    def pair_of(n, pr):
        sh = 4 - n
        low = ((pr >> sh) << (sh + 1)) + (pr & ((1 << sh) - 1))
        return low, low + (1 << sh)

    def state(n, blk, j):
        if n == 0:
            return hin[blk, 0 if j < 3 else 1].astype(F32)
        return st[n - 1, blk, j].astype(F32)

    for n in range(SEC):

        def forward(pr, n=n):
            t0, t1 = pair_of(n, pr)
            for j in range(4):
                a, b = state(n, t0, j), state(n, t1, j)
                cs, sn = ccos[n, pr, j], csin[n, pr, j]
                low = (cs * a - sn * b).astype(BF16)
                high = (sn * a + cs * b).astype(BF16)
                if n < SEC - 1:
                    st[n, t0, j] = low
                    st[n, t1, j] = high
                else:
                    h5s[t0, j] = low
                    h5s[t1, j] = high

        loop(0, 16, forward)

    def h5_copy(p, src):
        return send(h5s.at[p], h5t.at[:, mine(src), :], s2.at[0], r2.at[0], p)

    loop(1, N, lambda i: h5_copy(lax.rem(t + i, N), t).start())
    h5t[:, mine(t), :] = h5s[t]

    ag_col(0, 3)
    ag_col(1, 1)
    ag_near(0, 1)
    dequantize(packq, qs, wq, 4096, 2048)
    ag_col(1, 2)
    ag_near(0, 2)
    ag_near(1, 0)
    dequantize(packq, qs, wq, 6144, 2048)
    ag_near(0, 3)
    ag_far(0, 0)
    ag_col(1, 3)
    ag_far(0, 1)
    ag_far(0, 2)
    ag_near(1, 1)
    ag_far(0, 3)

    def narrow(j, w, first):
        piece = dot(hl[j], w[...]).astype(BF16)
        for i in range(8):
            turned = dot_nt(eye(TOK), piece[:, 128 * i : 128 * i + 128]).astype(BF16)
            for k in range(4):
                slot = ((k % 2) * 4 + 2 * (i % 2) + k // 2) * 4 + i // 2
                part[slot, first : first + 32, :] = turned[32 * k : 32 * k + 32, :]

    def wide(zp):
        def column(x_):
            cols = pl.ds(pl.multiple_of((x_ * 4 + zp) * 512, 512), 512)
            for j, w, first in ((0, wq, 0), (3, wo, 320)):
                piece = dot(hl[j], w[:, cols]).astype(BF16)
                for c_ in range(2):
                    for half in range(2):
                        at = c_ * 256 + half * 128
                        rows = slice(first + half * 128, first + half * 128 + 128)
                        part[(c_ * 4 + zp) * 4 + x_, rows, :] = piece[:, at : at + 128]

        loop(0, 4, column)

    def piece_z(p):
        return (3, 0, 2, 1)[p]

    def base(zp):
        return (c * 4 + zp) * 4

    def a_copy(p):
        zp = piece_z(p)
        return send(
            part.at[pl.ds(((1 - c) * 4 + zp) * 4, 4)], ra.at[pl.ds(zp * 4, 4)],
            ra_s.at[p], ra_r.at[p], sib,
        )

    def x1_copy(p, way):
        zp = piece_z(p)
        return send(
            part.at[base(zp) + x2, pl.ds(way * HALF, HALF), :], rx1.at[zp, way],
            rx1_s.at[2 * p + way], rx1_r.at[2 * p + way], dev(xm if way else xp, z, c),
        )

    def x2_copy(p, way):
        zp = piece_z(p)
        to = xm if way else xp
        return send(
            part.at[base(zp) + to], rx2.at[zp, way],
            rx2_s.at[2 * p + way], rx2_r.at[2 * p + way], dev(to, z, c),
        )

    def z_copy(dest, src):
        return send(
            accx.at[dest], rz.at[src], rz_s.at[dest], rz_r.at[src], dev(x, dest, c)
        )

    def stage_z(dest):
        pl.when(z != dest)(lambda: z_copy(dest, z).start())

    def stage_x1(p):
        zp = piece_z(p)
        a_copy(p).wait_recv()
        add_rows(part, base(zp) + x2, (0, ROWS), [(ra, (zp * 4 + x2,), 0)])
        x1_copy(p, 0).start()
        x1_copy(p, 1).start()
        for x_ in (xp, xm, x):
            add_rows(part, base(zp) + x_, (0, ROWS), [(ra, (zp * 4 + x_,), 0)])

    def stage_x2(p):
        zp = piece_z(p)
        x1_copy(p, 0).wait_recv()
        add_rows(part, base(zp) + xp, (0, HALF), [(rx1, (zp, 0), 0)])
        x2_copy(p, 0).start()
        x1_copy(p, 1).wait_recv()
        add_rows(part, base(zp) + xm, (HALF, ROWS), [(rx1, (zp, 1), 0)])
        x2_copy(p, 1).start()

    def stage_x3(p):
        zp = piece_z(p)
        x2_copy(p, 0).wait_recv()
        x2_copy(p, 1).wait_recv()
        add_rows(part, base(zp) + x, (0, ROWS), [(rx2, (zp, 0), 0), (rx2, (zp, 1), 0)], accx, zp)

    def back_wide(j, w, first):
        total = None
        for quarter in range(4):
            rhs = jnp.concatenate(
                [
                    ag[c_ * 16 + 4 * quarter + i, first : first + 256, :]
                    for i in range(4)
                    for c_ in range(2)
                ],
                axis=0,
            )
            piece = dot(w[:, 2048 * quarter : 2048 * quarter + 2048], rhs)
            if quarter == 0:
                acc[...] = piece
            elif quarter < 3:
                acc[...] += piece
            else:
                bks[j] = (acc[...] + piece).astype(BF16)

    def back_narrow(j, w, first):
        rhs = jnp.concatenate(
            [ag[c_ * 16 + i, first : first + 32, :] for i in range(16) for c_ in range(2)], axis=0
        )
        bks[j] = dot(w[...], rhs).astype(BF16)

    def back_copy(k, p, slot):
        js = pl.ds(0, 3) if k == 0 else pl.ds(3, 1)
        return send(
            bks.at[js, mine(p), :], bkr.at[slot, js], s3.at[k], r3.at[k], p
        )

    ag_own(0)
    back_wide(0, wq, 0)
    back_narrow(1, wk, 256)
    back_narrow(2, wv, 288)
    loop(1, N, lambda i: back_copy(0, lax.rem(t + i, N), t).start())
    bkr[t, 0:3] = bks[0:3, mine(t), :]
    loads[3].wait()
    dequantize(packo, os_, wo, 0, 4096)
    ag_near(1, 2)
    ag_near(1, 3)
    ag_far(1, 0)
    dequantize(packo, os_, wo, 4096, 4096)

    group(h5s, s2, r2).wait_recv()
    for j in range(4):
        hl[j] = dot_nt(eye(TOK), h5t[j]).astype(BF16)
    narrow(1, wk, 256)
    narrow(2, wv, 288)
    wide(piece_z(0))
    a_copy(0).start()
    wide(piece_z(1))
    a_copy(1).start()
    stage_x1(0)
    for k in (1, 2, 3):
        ag_far(1, k)
    ag_own(1)
    back_wide(3, wo, 320)
    loop(1, N, lambda i: back_copy(1, lax.rem(t + i, N), t).start())
    bkr[t, 3] = bks[3, mine(t), :]
    wide(piece_z(2))
    a_copy(2).start()
    stage_x1(1)
    stage_x2(0)
    wide(piece_z(3))
    a_copy(3).start()
    stage_x1(2)
    stage_x2(1)

    def backward_sections(js):
        for n in reversed(range(SEC)):
            take, put = (bkr, gb) if n % 2 == 0 else (gb, bkr)

            def backward(pr, grads, n=n, take=take, put=put):
                t0, t1 = pair_of(n, pr)
                lows, highs = [], []
                for j in js:
                    cs, sn = ccos[n, pr, j], csin[n, pr, j]
                    gl, gu = take[t0, j].astype(F32), take[t1, j].astype(F32)
                    low = cs * gl + sn * gu
                    high = cs * gu - sn * gl
                    e = state(n, t0, j) * high - state(n, t1, j) * low
                    total = jnp.sum(e, axis=1, keepdims=True) * (1.0 + cs)
                    grads = jnp.where(lanes == pr * 4 + j, total, grads)
                    lows.append(low)
                    highs.append(high)
                    if n:
                        put[t0, j] = low.astype(BF16)
                        put[t1, j] = high.astype(BF16)
                if n == 0:
                    for blk, parts in ((t0, lows), (t1, highs)):
                        whole = parts[0] + parts[1] + parts[2] if len(js) == 3 else parts[0]
                        gs[0 if len(js) == 3 else 1, blk] = whole.astype(BF16)
                return grads

            first = jnp.zeros((SUB, TOK), F32) if len(js) == 3 else angy[y, n]
            angy[y, n] = lax.fori_loop(0, 16, backward, first, unroll=BU)

    def out_copy(k, p, src):
        return send(gs.at[k, p], gt.at[k, mine(src), :], s4.at[k], r4.at[k], p)

    group(bkr.at[:, pl.ds(0, 3)], s3, r3).wait_recv()
    backward_sections((0, 1, 2))
    loop(1, N, lambda i: out_copy(0, lax.rem(t + i, N), t).start())
    stage_x1(3)
    stage_x2(2)
    stage_x3(0)
    stage_z(piece_z(0))
    group(bkr.at[:, pl.ds(3, 1)], s3, r3, 1).wait_recv()
    backward_sections((3,))

    def y_copy(k, slot):
        return send(angy.at[slot], angy.at[slot], sd.at[k], rd.at[slot], dp_peers[k], "dp")

    for k in range(3):
        y_copy(k, y).start()

    loop(1, N, lambda i: out_copy(1, lax.rem(t + i, N), t).start())
    for k in range(2):
        gt[k, mine(t), :] = gs[k, t]
    stage_x2(3)
    stage_x3(1)
    stage_z(piece_z(1))

    def far_copy(slot):
        return send(angz.at[slot], angz.at[slot], sd.at[3], rd.at[4], far, "dp")

    for k in range(3):
        y_copy(k, lax.rem(y + 1 + k, 4)).wait_recv()
    for n in range(SEC):
        angz[zh, n] = ((angy[0, n] + angy[1, n]) + angy[2, n]) + angy[3, n]
    far_copy(zh).start()
    stage_x3(2)
    stage_z(piece_z(2))
    stage_x3(3)
    stage_z(piece_z(3))

    far_copy(1 - zh).wait_recv()
    for n in range(SEC):
        whole = angz[0, n] + angz[1, n]
        for pr in range(16):
            moved = pltpu.roll(whole, (4 * n - 4 * pr) % TOK, 1)
            keep = (lanes >= 4 * n) & (lanes < 4 * n + 4)
            spread[n, pr] = jnp.where(keep, moved, 0.0)

    def message(blk):
        whole = jnp.zeros((SUB, TOK), F32)
        for n in range(SEC):
            sh = 4 - n
            whole = whole + spread[n, ((blk >> (sh + 1)) << sh) + (blk & ((1 << sh) - 1))]
        top = whole.astype(BF16).astype(F32)
        rest = pltpu.roll(whole - top, 32, 1)
        angs[blk] = jnp.where(lanes < 32, top, rest).astype(BF16)

    def ang_copy(p, src):
        return send(angs.at[p], angt.at[mine(src), :], s5.at[0], r5.at[0], p)

    loop(0, N, message, unroll=4)
    loop(1, N, lambda i: ang_copy(lax.rem(t + i, N), t).start())
    angt[mine(t), :] = angs[t]

    total = accx[z].astype(F32)
    for k in (1, 2, 3):
        z_copy(0, order[k]).wait_recv()
    for k in (1, 2, 3):
        total = total + rz[order[k]].astype(F32)
    total = total.astype(BF16)
    q_out[:, 0:128] = total[0:128]
    q_out[:, 128:256] = total[128:256]
    o_out[:, 0:128] = total[320:448]
    o_out[:, 128:256] = total[448:576]
    k_out[...] = total[256:288]
    v_out[...] = total[288:320]

    def natural(value):
        return dot(dot_nt(eye(TOK), value).astype(BF16), perm[...])

    group(gs.at[0], s4, r4).wait_recv()
    tg[...] = natural(gt[0]).astype(BF16)
    group(gs.at[1], s4, r4, 1).wait_recv()
    mg[...] = natural(gt[1]).astype(BF16)

    group(angs, s5, r5).wait_recv()
    both = natural(angt[...])
    ang_out[...] = both[0:32] + both[32:64]

    group(hin, s1, r1).wait_send()
    group(h5s, s2, r2).wait_send()
    group(bkr.at[:, pl.ds(0, 3)], s3, r3).wait_send()
    group(bkr.at[:, pl.ds(3, 1)], s3, r3, 1).wait_send()
    group(gs.at[0], s4, r4).wait_send()
    group(gs.at[1], s4, r4, 1).wait_send()
    group(angs, s5, r5).wait_send()
    for part_ in range(2):
        ag_z(part_, left)
        for k in (1, 2, 3):
            ag_on(part_, k, left)
        loop(5, 33, lambda i, p=part_: ag_copy(i, p, x, z, sib, ag_r).wait_send())
    for p in range(4):
        a_copy(p).wait_send()
        for way in range(2):
            x1_copy(p, way).wait_send()
            x2_copy(p, way).wait_send()
        pl.when(z != p)(lambda p=p: z_copy(p, z).wait_send())
    for k in range(3):
        y_copy(k, y).wait_send()
    far_copy(zh).wait_send()


def shards(*args):
    def vm(shape, dtype=BF16):
        return pltpu.VMEM(shape, dtype)

    def sem(n):
        return pltpu.SemaphoreType.DMA((n,))

    scratch = [
        vm((128, 8192), F32), vm((128, 1024), F32), vm((128, 1024), F32), vm((128, 8192), F32),
        vm((CH, 8192)), vm((CH, 1024)), vm((CH, 1024)), vm((CH, 8192)),
        vm((CH, CH)),
        vm((2, CH, TOK)), vm((N, 2, SUB, TOK)),
        vm((SEC - 1, N, 4, SUB, TOK)), vm((N, 4, SUB, TOK)),
        vm((4, CH, TOK)), vm((4, TOK, CH)),
        vm((SEC, 16, 4, SUB, TOK), F32), vm((SEC, 16, 4, SUB, TOK), F32),
        vm((N, ROWS, TOK)), vm((N, ROWS, TOK)),
        vm((16, ROWS, TOK)),
        vm((4, 2, HALF, TOK)), vm((4, 2, ROWS, TOK)),
        vm((4, ROWS, TOK)), vm((4, ROWS, TOK)),
        vm((CH, TOK), F32),
        vm((4, CH, TOK)), vm((N, 4, SUB, TOK)), vm((N, 4, SUB, TOK)),
        vm((2, N, SUB, TOK)), vm((2, CH, TOK)),
        vm((4, SEC, SUB, TOK), F32), vm((2, SEC, SUB, TOK), F32),
        vm((SEC, 16, SUB, TOK), F32), vm((N, SUB, TOK)), vm((CH, TOK)),
        sem(4), sem(1), sem(1), sem(1), sem(1), sem(2), sem(2), sem(2), sem(2),
        sem(66), sem(32), sem(32), sem(4), sem(4), sem(8), sem(8), sem(8), sem(8),
        sem(4), sem(4), sem(4), sem(5), sem(1), sem(1),
    ]
    shapes = [(TOK, 256), (32, TOK), (32, TOK), (TOK, 256), (TOK, CH), (TOK, CH)]
    outs = [jax.ShapeDtypeStruct(shape, BF16) for shape in shapes]
    in_vmem = pl.BlockSpec(memory_space=pltpu.VMEM)
    in_any = pl.BlockSpec(memory_space=pl.ANY)
    args = list(args)
    args[2] = args[2].transpose(1, 0, 2)
    args[12], args[13] = args[12].T, args[13].T
    results = pl.pallas_call(
        kernel,
        out_shape=outs + [jax.ShapeDtypeStruct((32, CH), F32)],
        in_specs=[in_any if i in (3, 5, 7, 9) else in_vmem for i in range(15)],
        out_specs=[in_vmem] * 7,
        scratch_shapes=scratch,
        compiler_params=pltpu.CompilerParams(
            collective_id=0, has_side_effects=True, vmem_limit_bytes=62 * 1024 * 1024
        ),
        cost_estimate=pl.CostEstimate(
            flops=4 * TOK * CH * 18432, bytes_accessed=12_000_000, transcendentals=0
        ),
    )(*args)

    def hand_over(*refs):
        for src, dst in zip(refs[:6], refs[7:13]):
            dst[...] = src[...]
        for n in range(SEC):
            refs[13][n] = refs[6][4 * n : 4 * n + 4, :]

    final = pl.pallas_call(
        hand_over,
        out_shape=outs + [jax.ShapeDtypeStruct((SEC, 4, CH), F32)],
        in_specs=[in_vmem] * 7,
        out_specs=[in_vmem] * 7,
    )(*results)
    q_out, k_out, v_out, o_out, tg, mg, ang = final
    return q_out, k_out.T, v_out.T, o_out, tg, mg, ang.transpose(1, 0, 2)


def solution(mesh):
    both = P("dp", "tensor")
    rows = P("tensor", None)
    return jax.shard_map(
        shards,
        mesh=mesh,
        in_specs=(both, both, P(), rows, rows, rows, rows, rows, rows, rows, rows)
        + (both, both, both, both),
        out_specs=(both, both, both, both, both, both, P(None, None, "tensor")),
        check_vma=False,
    )
```

```python
import jax
import jax.numpy as jnp
from jax import lax
from jax.experimental import pallas as pl
from jax.experimental.pallas import tpu as pltpu
from jax.sharding import PartitionSpec as P

F32 = jnp.float32
BF16 = jnp.bfloat16
MESH = pl.DeviceIdType.MESH
N = 32
BU = 2
CH = 512
SUB = 16
TOK = 128
SEC = 5
ROWS = 576
HALF = 288
PARTS = (pl.ds(0, 320), pl.ds(320, 256))
NT = (((1,), (1,)), ((), ()))


def dot(a, b):
    return jnp.dot(a, b, preferred_element_type=F32)


def dot_nt(a, b):
    return lax.dot_general(a, b, NT, preferred_element_type=F32)


def eye(n):
    r = lax.broadcasted_iota(jnp.int32, (n, n), 0)
    c = lax.broadcasted_iota(jnp.int32, (n, n), 1)
    return jnp.where(r == c, 1.0, 0.0).astype(BF16)


def loop(lo, hi, fn, unroll=1):
    def step(i, carry):
        fn(i)
        return carry

    lax.fori_loop(lo, hi, step, 0, unroll=unroll)


def dequantize(packed, scale, out, first, width):
    def chunk(i):
        cols = pl.ds(pl.multiple_of(first + i * 128, 128), 128)
        spread = scale[:, cols].astype(F32)
        for g in range(8):
            rows = slice(16 * g, 16 * g + 16)
            word = packed[rows, cols].astype(jnp.int32)
            s = jnp.broadcast_to(spread[g : g + 1, :], (16, 128))
            for plane in range(4):
                digit = (word >> (4 * plane)) & 15 if plane < 3 else word >> 12
                value = (digit.astype(F32) - 7.5) * s
                out[128 * plane + 16 * g : 128 * plane + 16 * g + 16, cols] = value.astype(BF16)

    loop(0, width // 128, chunk)


def add_rows(dst, base, rows, srcs, out=None, out_base=0):
    def step(i):
        off = pl.multiple_of(i * 96, 96)
        total = dst[base, pl.ds(rows[0] + off, 96), :].astype(F32)
        for ref, index, first in srcs:
            total = total + ref[index + (pl.ds(first + off, 96), slice(None))].astype(F32)
        if out is None:
            dst[base, pl.ds(rows[0] + off, 96), :] = total.astype(BF16)
        else:
            out[out_base, pl.ds(rows[0] + off, 96), :] = total.astype(BF16)

    loop(0, (rows[1] - rows[0]) // 96, step)


def kernel(
    tok, mix, ang, qp, qs, kp, ks, vp, vs, op, os_, qc, kc, vc, oc,
    q_out, k_out, v_out, o_out, tg, mg, ang_out,
    packq, packk, packv, packo, wq, wk, wv, wo, perm,
    angv, tok_t, hin, st, h5s, h5t, hl, ccos, csin,
    ag, part, ra, rx1, rx2, accx, rz, acc, bks, bkr, gb, gs, gt, angy, angz, spread, angs, angt,
    ld, s1, r1, s2, r2, s3, r3, s4, r4, ag_s, ag_r, ag_sib, ra_s, ra_r, rx1_s, rx1_r,
    rx2_s, rx2_r, rz_s, rz_r, sd, rd, s5, r5,
):
    d = lax.axis_index("dp")
    t = lax.axis_index("tensor")
    x = lax.div(t, 8)
    z = lax.rem(lax.div(t, 2), 4)
    c = lax.rem(t, 2)
    xp, xm, x2 = lax.rem(x + 1, 4), lax.rem(x + 3, 4), lax.rem(x + 2, 4)

    def dev(x_, z_, c_):
        return (x_ * 4 + z_) * 2 + c_

    sib = dev(x, z, 1 - c)
    y, zh = lax.div(d, 2), lax.rem(d, 2)
    far = y * 2 + 1 - zh
    dp_peers = [lax.rem(y + i, 4) * 2 + zh for i in (1, 2, 3)] + [far]

    def send(src, dst, ssem, rsem, peer, axis="tensor"):
        return pltpu.make_async_remote_copy(
            src_ref=src, dst_ref=dst, send_sem=ssem, recv_sem=rsem,
            device_id={axis: peer}, device_id_type=MESH,
        )

    bar = pltpu.get_barrier_semaphore()
    loop(1, N, lambda i: pl.semaphore_signal(
        bar, inc=1, device_id={"tensor": lax.rem(t + i, N)}, device_id_type=MESH))
    for peer in dp_peers:
        pl.semaphore_signal(bar, inc=1, device_id={"dp": peer}, device_id_type=MESH)

    loads = [
        pltpu.make_async_copy(src, dst, ld.at[i])
        for i, (src, dst) in enumerate(((kp, packk), (vp, packv), (qp, packq), (op, packo), (ang, angv)))
    ]
    for i in (4, 0, 1, 2, 3):
        loads[i].start()
    r = lax.broadcasted_iota(jnp.int32, (CH, CH), 0)
    col = lax.broadcasted_iota(jnp.int32, (CH, CH), 1)
    perm[...] = jnp.where(col == 4 * (r & 127) + (r >> 7), 1.0, 0.0).astype(BF16)
    tok_t[0] = dot_nt(perm[...], tok[...]).astype(BF16)
    tok_t[1] = dot_nt(perm[...], mix[...]).astype(BF16)
    own = c * 16 + x * 4 + z
    ag[own, 0:256, :] = dot_nt(eye(256), qc[...]).astype(BF16)
    ag[own, 320:576, :] = dot_nt(eye(256), oc[...]).astype(BF16)
    ag[own, 256:288, :] = kc[...]
    ag[own, 288:320, :] = vc[...]
    pl.semaphore_wait(bar, N - 1 + 4)

    def mine(p):
        return pl.ds(pl.multiple_of(p * SUB, SUB), SUB)

    def group(ref, ssem, rsem, k=0):
        all_ = ref.at[pl.ds(0, N - 1)]
        return send(all_, all_, ssem.at[k], rsem.at[k], sib)

    def in_copy(p, slot):
        return send(tok_t.at[:, mine(p), :], hin.at[slot], s1.at[0], r1.at[0], p)

    near = z - 1 + 2 * lax.div(3 - z, 3)
    last = 3 * (1 - lax.div(z, 2))
    order = (z, near, 6 - z - near - last, last)

    def ag_copy(k, part_, x_, z_, peer, sems):
        here = ag.at[c * 16 + x_ * 4 + z_, PARTS[part_], :]
        at = part_ * 16 + x_ * 4 + z_
        return send(here, here, ag_s.at[part_ * 33 + k], sems.at[at], peer)

    def ag_wait(part_, x_, z_):
        ag_copy(0, part_, x_, z_, sib, ag_r).wait_recv()

    def upward(part_, k, z_):
        return ag_copy(k, part_, x, z_, dev(x, z + 1, c), ag_r)

    def downward(part_, k, z_):
        return ag_copy(k, part_, x, z_, dev(x, z - 1, c), ag_r)

    def ag_z(part_, act):
        @pl.when(z < 3)
        def _():
            act(upward(part_, 0, z))

        @pl.when(z > 0)
        def _():
            act(downward(part_, 1, z))

    def ag_on(part_, k, act):
        @pl.when((order[k] < z) & (z < 3))
        def _():
            act(upward(part_, 1 + k, order[k]))

        @pl.when((order[k] > z) & (z > 0))
        def _():
            act(downward(part_, 1 + k, order[k]))

    def start(copy):
        copy.start()

    def left(copy):
        copy.wait_send()

    def ag_row(part_, k):
        ag_copy(5 + 2 * k, part_, x, order[k], dev(xp, z, c), ag_r).start()
        ag_copy(6 + 2 * k, part_, x, order[k], dev(xm, z, c), ag_r).start()
        ag_copy(17 + k, part_, x, order[k], sib, ag_sib).start()

    def ag_col(part_, k):
        ag_wait(part_, x, order[k])
        ag_on(part_, k, start)
        ag_row(part_, k)

    def ag_near(part_, k):
        ag_wait(part_, xm, order[k])
        if k % 2 == 0:
            ag_copy(13 + k, part_, xm, order[k], dev(xp, z, c), ag_r).start()
        ag_copy(21 + k, part_, xm, order[k], sib, ag_sib).start()
        ag_wait(part_, xp, order[k])
        if k % 2 == 1:
            ag_copy(13 + k, part_, xp, order[k], dev(xm, z, c), ag_r).start()
        ag_copy(25 + k, part_, xp, order[k], sib, ag_sib).start()

    def ag_far(part_, k):
        ag_wait(part_, x2, order[k])
        ag_copy(29 + k, part_, x2, order[k], sib, ag_sib).start()

    def ag_own(part_):
        for x_ in range(4):
            for z_ in range(4):
                here = ag.at[(1 - c) * 16 + x_ * 4 + z_, PARTS[part_], :]
                at = part_ * 16 + x_ * 4 + z_
                send(here, here, ag_s.at[0], ag_sib.at[at], sib).wait_recv()

    ag_z(0, start)
    ag_row(0, 0)
    loop(1, N, lambda i: in_copy(lax.rem(t + i, N), t).start())
    hin[t] = tok_t[:, mine(t), :]
    ag_z(1, start)
    ag_row(1, 0)

    lanes = lax.broadcasted_iota(jnp.int32, (SUB, TOK), 1)
    subs = lax.broadcasted_iota(jnp.int32, (SUB, TOK), 0)
    pick = lanes == 4 * subs + (64 * c + x)
    window = 128 * lax.div(lax.rem(t, 8), 2)

    loads[4].wait()

    def factors(pr):
        where = pl.ds(pl.multiple_of(pr * CH + window, 128), 128)
        for j in range(4):
            for n in range(SEC):
                row = jnp.broadcast_to(angv[n, j : j + 1, where], (SUB, TOK))
                angle = jnp.sum(jnp.where(pick, row, 0.0), axis=1, keepdims=True)
                square = angle * angle
                inverse = 1.0 / (1.0 + square)
                ccos[n, pr, j] = jnp.broadcast_to((1.0 - square) * inverse, (SUB, TOK))
                csin[n, pr, j] = jnp.broadcast_to(2.0 * angle * inverse, (SUB, TOK))

    loop(0, 16, factors)
    loads[0].wait()
    dequantize(packk, ks, wk, 0, 1024)
    loads[1].wait()
    dequantize(packv, vs, wv, 0, 1024)

    loads[2].wait()
    dequantize(packq, qs, wq, 0, 2048)
    ag_col(0, 1)
    dequantize(packq, qs, wq, 2048, 2048)
    ag_near(0, 0)
    ag_col(0, 2)

    group(hin, s1, r1).wait_recv()

    def pair_of(n, pr):
        sh = 4 - n
        low = ((pr >> sh) << (sh + 1)) + (pr & ((1 << sh) - 1))
        return low, low + (1 << sh)

    def state(n, blk, j):
        if n == 0:
            return hin[blk, 0 if j < 3 else 1].astype(F32)
        return st[n - 1, blk, j].astype(F32)

    for n in range(SEC):

        def forward(pr, n=n):
            t0, t1 = pair_of(n, pr)
            for j in range(4):
                a, b = state(n, t0, j), state(n, t1, j)
                cs, sn = ccos[n, pr, j], csin[n, pr, j]
                low = (cs * a - sn * b).astype(BF16)
                high = (sn * a + cs * b).astype(BF16)
                if n < SEC - 1:
                    st[n, t0, j] = low
                    st[n, t1, j] = high
                else:
                    h5s[t0, j] = low
                    h5s[t1, j] = high

        loop(0, 16, forward)

    def h5_copy(p, src):
        return send(h5s.at[p], h5t.at[:, mine(src), :], s2.at[0], r2.at[0], p)


    ag_col(0, 3)
    ag_col(1, 1)
    ag_near(0, 1)
    dequantize(packq, qs, wq, 4096, 2048)
    ag_col(1, 2)
    loop(1, N, lambda i: h5_copy(lax.rem(t + i, N), t).start())
    h5t[:, mine(t), :] = h5s[t]
    ag_near(0, 2)
    ag_near(1, 0)
    dequantize(packq, qs, wq, 6144, 2048)
    ag_near(0, 3)
    ag_far(0, 0)
    ag_col(1, 3)
    ag_far(0, 1)
    ag_far(0, 2)
    ag_near(1, 1)
    ag_far(0, 3)

    def narrow(j, w, first):
        piece = dot(hl[j], w[...]).astype(BF16)
        for i in range(8):
            turned = dot_nt(eye(TOK), piece[:, 128 * i : 128 * i + 128]).astype(BF16)
            for k in range(4):
                slot = ((k % 2) * 4 + 2 * (i % 2) + k // 2) * 4 + i // 2
                part[slot, first : first + 32, :] = turned[32 * k : 32 * k + 32, :]

    def wide(zp):
        def column(x_):
            cols = pl.ds(pl.multiple_of((x_ * 4 + zp) * 512, 512), 512)
            for j, w, first in ((0, wq, 0), (3, wo, 320)):
                piece = dot(hl[j], w[:, cols]).astype(BF16)
                for c_ in range(2):
                    for half in range(2):
                        at = c_ * 256 + half * 128
                        rows = slice(first + half * 128, first + half * 128 + 128)
                        part[(c_ * 4 + zp) * 4 + x_, rows, :] = piece[:, at : at + 128]

        loop(0, 4, column)

    def piece_z(p):
        return (3, 0, 2, 1)[p]

    def base(zp):
        return (c * 4 + zp) * 4

    def a_copy(p):
        zp = piece_z(p)
        return send(
            part.at[pl.ds(((1 - c) * 4 + zp) * 4, 4)], ra.at[pl.ds(zp * 4, 4)],
            ra_s.at[p], ra_r.at[p], sib,
        )

    def x1_copy(p, way):
        zp = piece_z(p)
        return send(
            part.at[base(zp) + x2, pl.ds(way * HALF, HALF), :], rx1.at[zp, way],
            rx1_s.at[2 * p + way], rx1_r.at[2 * p + way], dev(xm if way else xp, z, c),
        )

    def x2_copy(p, way):
        zp = piece_z(p)
        to = xm if way else xp
        return send(
            part.at[base(zp) + to], rx2.at[zp, way],
            rx2_s.at[2 * p + way], rx2_r.at[2 * p + way], dev(to, z, c),
        )

    def z_copy(dest, src):
        return send(
            accx.at[dest], rz.at[src], rz_s.at[dest], rz_r.at[src], dev(x, dest, c)
        )

    def stage_z(dest):
        pl.when(z != dest)(lambda: z_copy(dest, z).start())

    def stage_x1(p):
        zp = piece_z(p)
        a_copy(p).wait_recv()
        add_rows(part, base(zp) + x2, (0, ROWS), [(ra, (zp * 4 + x2,), 0)])
        x1_copy(p, 0).start()
        x1_copy(p, 1).start()
        for x_ in (xp, xm, x):
            add_rows(part, base(zp) + x_, (0, ROWS), [(ra, (zp * 4 + x_,), 0)])

    def stage_x2(p):
        zp = piece_z(p)
        x1_copy(p, 0).wait_recv()
        add_rows(part, base(zp) + xp, (0, HALF), [(rx1, (zp, 0), 0)])
        x2_copy(p, 0).start()
        x1_copy(p, 1).wait_recv()
        add_rows(part, base(zp) + xm, (HALF, ROWS), [(rx1, (zp, 1), 0)])
        x2_copy(p, 1).start()

    def stage_x3(p):
        zp = piece_z(p)
        x2_copy(p, 0).wait_recv()
        x2_copy(p, 1).wait_recv()
        add_rows(part, base(zp) + x, (0, ROWS), [(rx2, (zp, 0), 0), (rx2, (zp, 1), 0)], accx, zp)

    def back_wide(j, w, first):
        total = None
        for quarter in range(4):
            rhs = jnp.concatenate(
                [
                    ag[c_ * 16 + 4 * quarter + i, first : first + 256, :]
                    for i in range(4)
                    for c_ in range(2)
                ],
                axis=0,
            )
            piece = dot(w[:, 2048 * quarter : 2048 * quarter + 2048], rhs)
            if quarter == 0:
                acc[...] = piece
            elif quarter < 3:
                acc[...] += piece
            else:
                bks[j] = (acc[...] + piece).astype(BF16)

    def back_narrow(j, w, first):
        rhs = jnp.concatenate(
            [ag[c_ * 16 + i, first : first + 32, :] for i in range(16) for c_ in range(2)], axis=0
        )
        bks[j] = dot(w[...], rhs).astype(BF16)

    def back_copy(k, p, slot):
        js = pl.ds(0, 3) if k == 0 else pl.ds(3, 1)
        return send(
            bks.at[js, mine(p), :], bkr.at[slot, js], s3.at[k], r3.at[k], p
        )

    ag_own(0)
    back_wide(0, wq, 0)
    back_narrow(1, wk, 256)
    back_narrow(2, wv, 288)
    loop(1, N, lambda i: back_copy(0, lax.rem(t + i, N), t).start())
    bkr[t, 0:3] = bks[0:3, mine(t), :]
    loads[3].wait()
    dequantize(packo, os_, wo, 0, 4096)
    ag_near(1, 2)
    ag_near(1, 3)
    ag_far(1, 0)
    dequantize(packo, os_, wo, 4096, 4096)

    group(h5s, s2, r2).wait_recv()
    for j in range(4):
        hl[j] = dot_nt(eye(TOK), h5t[j]).astype(BF16)
    narrow(1, wk, 256)
    narrow(2, wv, 288)
    wide(piece_z(0))
    a_copy(0).start()
    wide(piece_z(1))
    a_copy(1).start()
    stage_x1(0)
    for k in (1, 2, 3):
        ag_far(1, k)
    wide(piece_z(2))
    a_copy(2).start()
    stage_x1(1)
    ag_own(1)
    back_wide(3, wo, 320)
    loop(1, N, lambda i: back_copy(1, lax.rem(t + i, N), t).start())
    bkr[t, 3] = bks[3, mine(t), :]
    stage_x2(0)
    wide(piece_z(3))
    a_copy(3).start()
    stage_x1(2)
    stage_x2(1)

    def backward_sections(js):
        for n in reversed(range(SEC)):
            take, put = (bkr, gb) if n % 2 == 0 else (gb, bkr)

            def backward(pr, grads, n=n, take=take, put=put):
                t0, t1 = pair_of(n, pr)
                lows, highs = [], []
                for j in js:
                    cs, sn = ccos[n, pr, j], csin[n, pr, j]
                    gl, gu = take[t0, j].astype(F32), take[t1, j].astype(F32)
                    low = cs * gl + sn * gu
                    high = cs * gu - sn * gl
                    e = state(n, t0, j) * high - state(n, t1, j) * low
                    total = jnp.sum(e, axis=1, keepdims=True) * (1.0 + cs)
                    grads = jnp.where(lanes == pr * 4 + j, total, grads)
                    lows.append(low)
                    highs.append(high)
                    if n:
                        put[t0, j] = low.astype(BF16)
                        put[t1, j] = high.astype(BF16)
                if n == 0:
                    for blk, parts in ((t0, lows), (t1, highs)):
                        whole = parts[0] + parts[1] + parts[2] if len(js) == 3 else parts[0]
                        gs[0 if len(js) == 3 else 1, blk] = whole.astype(BF16)
                return grads

            first = jnp.zeros((SUB, TOK), F32) if len(js) == 3 else angy[y, n]
            angy[y, n] = lax.fori_loop(0, 16, backward, first, unroll=BU)

    def out_copy(k, p, src):
        return send(gs.at[k, p], gt.at[k, mine(src), :], s4.at[k], r4.at[k], p)

    group(bkr.at[:, pl.ds(0, 3)], s3, r3).wait_recv()
    backward_sections((0, 1, 2))
    loop(1, N, lambda i: out_copy(0, lax.rem(t + i, N), t).start())
    stage_x1(3)
    stage_x2(2)
    stage_x3(0)
    stage_z(piece_z(0))
    group(bkr.at[:, pl.ds(3, 1)], s3, r3, 1).wait_recv()
    backward_sections((3,))

    def y_copy(k, slot):
        return send(angy.at[slot], angy.at[slot], sd.at[k], rd.at[slot], dp_peers[k], "dp")

    for k in range(3):
        y_copy(k, y).start()

    loop(1, N, lambda i: out_copy(1, lax.rem(t + i, N), t).start())
    for k in range(2):
        gt[k, mine(t), :] = gs[k, t]
    stage_x2(3)
    stage_x3(1)
    stage_z(piece_z(1))

    def far_copy(slot):
        return send(angz.at[slot], angz.at[slot], sd.at[3], rd.at[4], far, "dp")

    for k in range(3):
        y_copy(k, lax.rem(y + 1 + k, 4)).wait_recv()
    for n in range(SEC):
        angz[zh, n] = ((angy[0, n] + angy[1, n]) + angy[2, n]) + angy[3, n]
    far_copy(zh).start()
    stage_x3(2)
    stage_z(piece_z(2))
    stage_x3(3)
    stage_z(piece_z(3))

    far_copy(1 - zh).wait_recv()
    for n in range(SEC):
        whole = angz[0, n] + angz[1, n]
        for pr in range(16):
            moved = pltpu.roll(whole, (4 * n - 4 * pr) % TOK, 1)
            keep = (lanes >= 4 * n) & (lanes < 4 * n + 4)
            spread[n, pr] = jnp.where(keep, moved, 0.0)

    def message(blk):
        whole = jnp.zeros((SUB, TOK), F32)
        for n in range(SEC):
            sh = 4 - n
            whole = whole + spread[n, ((blk >> (sh + 1)) << sh) + (blk & ((1 << sh) - 1))]
        top = whole.astype(BF16).astype(F32)
        rest = pltpu.roll(whole - top, 32, 1)
        angs[blk] = jnp.where(lanes < 32, top, rest).astype(BF16)

    def ang_copy(p, src):
        return send(angs.at[p], angt.at[mine(src), :], s5.at[0], r5.at[0], p)

    loop(0, N, message, unroll=4)
    loop(1, N, lambda i: ang_copy(lax.rem(t + i, N), t).start())
    angt[mine(t), :] = angs[t]

    total = accx[z].astype(F32)
    for k in (1, 2, 3):
        z_copy(0, order[k]).wait_recv()
    for k in (1, 2, 3):
        total = total + rz[order[k]].astype(F32)
    total = total.astype(BF16)
    q_out[:, 0:128] = total[0:128]
    q_out[:, 128:256] = total[128:256]
    o_out[:, 0:128] = total[320:448]
    o_out[:, 128:256] = total[448:576]
    k_out[...] = total[256:288]
    v_out[...] = total[288:320]

    def natural(value):
        return dot(dot_nt(eye(TOK), value).astype(BF16), perm[...])

    group(gs.at[0], s4, r4).wait_recv()
    tg[...] = natural(gt[0]).astype(BF16)
    group(gs.at[1], s4, r4, 1).wait_recv()
    mg[...] = natural(gt[1]).astype(BF16)

    group(hin, s1, r1).wait_send()
    group(h5s, s2, r2).wait_send()
    group(bkr.at[:, pl.ds(0, 3)], s3, r3).wait_send()
    group(bkr.at[:, pl.ds(3, 1)], s3, r3, 1).wait_send()
    group(gs.at[0], s4, r4).wait_send()
    group(gs.at[1], s4, r4, 1).wait_send()
    for part_ in range(2):
        ag_z(part_, left)
        for k in (1, 2, 3):
            ag_on(part_, k, left)
        loop(5, 33, lambda i, p=part_: ag_copy(i, p, x, z, sib, ag_r).wait_send())
    for p in range(4):
        a_copy(p).wait_send()
        for way in range(2):
            x1_copy(p, way).wait_send()
            x2_copy(p, way).wait_send()
        pl.when(z != p)(lambda p=p: z_copy(p, z).wait_send())
    for k in range(3):
        y_copy(k, y).wait_send()
    far_copy(zh).wait_send()

    group(angs, s5, r5).wait_recv()
    both = dot(dot_nt(eye(TOK)[0:64], angt[...]).astype(BF16), perm[...])
    ang_out[...] = both[0:32] + both[32:64]
    group(angs, s5, r5).wait_send()


def shards(*args):
    def vm(shape, dtype=BF16):
        return pltpu.VMEM(shape, dtype)

    def sem(n):
        return pltpu.SemaphoreType.DMA((n,))

    scratch = [
        vm((128, 8192), F32), vm((128, 1024), F32), vm((128, 1024), F32), vm((128, 8192), F32),
        vm((CH, 8192)), vm((CH, 1024)), vm((CH, 1024)), vm((CH, 8192)),
        vm((CH, CH)),
        vm((SEC, 4, 8192), F32), vm((2, CH, TOK)), vm((N, 2, SUB, TOK)),
        vm((SEC - 1, N, 4, SUB, TOK)), vm((N, 4, SUB, TOK)),
        vm((4, CH, TOK)), vm((4, TOK, CH)),
        vm((SEC, 16, 4, SUB, TOK), F32), vm((SEC, 16, 4, SUB, TOK), F32),
        vm((N, ROWS, TOK)), vm((N, ROWS, TOK)),
        vm((16, ROWS, TOK)),
        vm((4, 2, HALF, TOK)), vm((4, 2, ROWS, TOK)),
        vm((4, ROWS, TOK)), vm((4, ROWS, TOK)),
        vm((CH, TOK), F32),
        vm((4, CH, TOK)), vm((N, 4, SUB, TOK)), vm((N, 4, SUB, TOK)),
        vm((2, N, SUB, TOK)), vm((2, CH, TOK)),
        vm((4, SEC, SUB, TOK), F32), vm((2, SEC, SUB, TOK), F32),
        vm((SEC, 16, SUB, TOK), F32), vm((N, SUB, TOK)), vm((CH, TOK)),
        sem(5), sem(1), sem(1), sem(1), sem(1), sem(2), sem(2), sem(2), sem(2),
        sem(66), sem(32), sem(32), sem(4), sem(4), sem(8), sem(8), sem(8), sem(8),
        sem(4), sem(4), sem(4), sem(5), sem(1), sem(1),
    ]
    shapes = [(TOK, 256), (32, TOK), (32, TOK), (TOK, 256), (TOK, CH), (TOK, CH)]
    outs = [jax.ShapeDtypeStruct(shape, BF16) for shape in shapes]
    in_vmem = pl.BlockSpec(memory_space=pltpu.VMEM)
    in_any = pl.BlockSpec(memory_space=pl.ANY)
    args = list(args)
    args[2] = args[2].transpose(1, 0, 2)
    args[12], args[13] = args[12].T, args[13].T
    results = pl.pallas_call(
        kernel,
        out_shape=outs + [jax.ShapeDtypeStruct((32, CH), F32)],
        in_specs=[in_any if i in (2, 3, 5, 7, 9) else in_vmem for i in range(15)],
        out_specs=[in_vmem] * 7,
        scratch_shapes=scratch,
        compiler_params=pltpu.CompilerParams(
            collective_id=0, has_side_effects=True, vmem_limit_bytes=62 * 1024 * 1024
        ),
        cost_estimate=pl.CostEstimate(
            flops=4 * TOK * CH * 18432, bytes_accessed=12_000_000, transcendentals=0
        ),
    )(*args)

    def hand_over(*refs):
        for src, dst in zip(refs[:6], refs[7:13]):
            dst[...] = src[...]
        for n in range(SEC):
            refs[13][n] = refs[6][4 * n : 4 * n + 4, :]

    final = pl.pallas_call(
        hand_over,
        out_shape=outs + [jax.ShapeDtypeStruct((SEC, 4, CH), F32)],
        in_specs=[in_vmem] * 7,
        out_specs=[in_vmem] * 7,
    )(*results)
    q_out, k_out, v_out, o_out, tg, mg, ang = final
    return q_out, k_out.T, v_out.T, o_out, tg, mg, ang.transpose(1, 0, 2)


def solution(mesh):
    both = P("dp", "tensor")
    rows = P("tensor", None)
    return jax.shard_map(
        shards,
        mesh=mesh,
        in_specs=(both, both, P(), rows, rows, rows, rows, rows, rows, rows, rows)
        + (both, both, both, both),
        out_specs=(both, both, both, both, both, both, P(None, None, "tensor")),
        check_vma=False,
    )
```

```python
import jax
import jax.numpy as jnp
from jax import lax
from jax.experimental import pallas as pl
from jax.experimental.pallas import tpu as pltpu
from jax.sharding import PartitionSpec as P

F32 = jnp.float32
BF16 = jnp.bfloat16
MESH = pl.DeviceIdType.MESH
N = 32
BU = 2
CH = 512
SUB = 16
TOK = 128
SEC = 5
ROWS = 576
HALF = 288
PARTS = (pl.ds(0, 320), pl.ds(320, 256))
NT = (((1,), (1,)), ((), ()))


def dot(a, b):
    return jnp.dot(a, b, preferred_element_type=F32)


def dot_nt(a, b):
    return lax.dot_general(a, b, NT, preferred_element_type=F32)


def eye(n):
    r = lax.broadcasted_iota(jnp.int32, (n, n), 0)
    c = lax.broadcasted_iota(jnp.int32, (n, n), 1)
    return jnp.where(r == c, 1.0, 0.0).astype(BF16)


def loop(lo, hi, fn, unroll=1):
    def step(i, carry):
        fn(i)
        return carry

    lax.fori_loop(lo, hi, step, 0, unroll=unroll)


def dequantize(packed, scale, out, first, width):
    def chunk(i):
        cols = pl.ds(pl.multiple_of(first + i * 128, 128), 128)
        spread = scale[:, cols].astype(F32)
        for g in range(8):
            rows = slice(16 * g, 16 * g + 16)
            word = packed[rows, cols].astype(jnp.int32)
            s = jnp.broadcast_to(spread[g : g + 1, :], (16, 128))
            for plane in range(4):
                digit = (word >> (4 * plane)) & 15 if plane < 3 else word >> 12
                value = (digit.astype(F32) - 7.5) * s
                out[128 * plane + 16 * g : 128 * plane + 16 * g + 16, cols] = value.astype(BF16)

    loop(0, width // 128, chunk)


def add_rows(dst, base, rows, srcs, out=None, out_base=0):
    def step(i):
        off = pl.multiple_of(i * 96, 96)
        total = dst[base, pl.ds(rows[0] + off, 96), :].astype(F32)
        for ref, index, first in srcs:
            total = total + ref[index + (pl.ds(first + off, 96), slice(None))].astype(F32)
        if out is None:
            dst[base, pl.ds(rows[0] + off, 96), :] = total.astype(BF16)
        else:
            out[out_base, pl.ds(rows[0] + off, 96), :] = total.astype(BF16)

    loop(0, (rows[1] - rows[0]) // 96, step)


def kernel(
    tok, mix, ang, qp, qs, kp, ks, vp, vs, op, os_, qc, kc, vc, oc,
    q_out, k_out, v_out, o_out, tg, mg, ang_out,
    packq, packk, packv, packo, wq, wk, wv, wo, perm,
    angv, tok_t, hin, st, h5s, h5t, hl, ccos, csin,
    ag, part, ra, rx1, rx2, accx, rz, acc, bks, bkr, gb, gs, gt, angy, angz, spread, angs, angt,
    ld, s1, r1, s2, r2, s3, r3, s4, r4, ag_s, ag_r, ag_sib, ra_s, ra_r, rx1_s, rx1_r,
    rx2_s, rx2_r, rz_s, rz_r, sd, rd, s5, r5,
):
    d = lax.axis_index("dp")
    t = lax.axis_index("tensor")
    x = lax.div(t, 8)
    z = lax.rem(lax.div(t, 2), 4)
    c = lax.rem(t, 2)
    xp, xm, x2 = lax.rem(x + 1, 4), lax.rem(x + 3, 4), lax.rem(x + 2, 4)

    def dev(x_, z_, c_):
        return (x_ * 4 + z_) * 2 + c_

    sib = dev(x, z, 1 - c)
    y, zh = lax.div(d, 2), lax.rem(d, 2)
    far = y * 2 + 1 - zh
    dp_peers = [lax.rem(y + i, 4) * 2 + zh for i in (1, 2, 3)] + [far]

    def send(src, dst, ssem, rsem, peer, axis="tensor"):
        return pltpu.make_async_remote_copy(
            src_ref=src, dst_ref=dst, send_sem=ssem, recv_sem=rsem,
            device_id={axis: peer}, device_id_type=MESH,
        )

    bar = pltpu.get_barrier_semaphore()
    loop(1, N, lambda i: pl.semaphore_signal(
        bar, inc=1, device_id={"tensor": lax.rem(t + i, N)}, device_id_type=MESH))
    for peer in dp_peers:
        pl.semaphore_signal(bar, inc=1, device_id={"dp": peer}, device_id_type=MESH)

    loads = [
        pltpu.make_async_copy(src, dst, ld.at[i])
        for i, (src, dst) in enumerate(((kp, packk), (vp, packv), (qp, packq), (op, packo), (ang, angv)))
    ]
    for i in (4, 0, 1, 2, 3):
        loads[i].start()
    r = lax.broadcasted_iota(jnp.int32, (CH, CH), 0)
    col = lax.broadcasted_iota(jnp.int32, (CH, CH), 1)
    perm[...] = jnp.where(col == 4 * (r & 127) + (r >> 7), 1.0, 0.0).astype(BF16)
    tok_t[0] = dot_nt(perm[...], tok[...]).astype(BF16)
    tok_t[1] = dot_nt(perm[...], mix[...]).astype(BF16)
    own = c * 16 + x * 4 + z
    ag[own, 0:256, :] = dot_nt(eye(256), qc[...]).astype(BF16)
    ag[own, 320:576, :] = dot_nt(eye(256), oc[...]).astype(BF16)
    ag[own, 256:288, :] = kc[...]
    ag[own, 288:320, :] = vc[...]
    pl.semaphore_wait(bar, N - 1 + 4)

    def mine(p):
        return pl.ds(pl.multiple_of(p * SUB, SUB), SUB)

    def group(ref, ssem, rsem, k=0):
        all_ = ref.at[pl.ds(0, N - 1)]
        return send(all_, all_, ssem.at[k], rsem.at[k], sib)

    def in_copy(p, slot):
        return send(tok_t.at[:, mine(p), :], hin.at[slot], s1.at[0], r1.at[0], p)

    near = z - 1 + 2 * lax.div(3 - z, 3)
    last = 3 * (1 - lax.div(z, 2))
    order = (z, near, 6 - z - near - last, last)

    def ag_copy(k, part_, x_, z_, peer, sems):
        here = ag.at[c * 16 + x_ * 4 + z_, PARTS[part_], :]
        at = part_ * 16 + x_ * 4 + z_
        return send(here, here, ag_s.at[part_ * 33 + k], sems.at[at], peer)

    def ag_wait(part_, x_, z_):
        ag_copy(0, part_, x_, z_, sib, ag_r).wait_recv()

    def upward(part_, k, z_):
        return ag_copy(k, part_, x, z_, dev(x, z + 1, c), ag_r)

    def downward(part_, k, z_):
        return ag_copy(k, part_, x, z_, dev(x, z - 1, c), ag_r)

    def ag_z(part_, act):
        @pl.when(z < 3)
        def _():
            act(upward(part_, 0, z))

        @pl.when(z > 0)
        def _():
            act(downward(part_, 1, z))

    def ag_on(part_, k, act):
        @pl.when((order[k] < z) & (z < 3))
        def _():
            act(upward(part_, 1 + k, order[k]))

        @pl.when((order[k] > z) & (z > 0))
        def _():
            act(downward(part_, 1 + k, order[k]))

    def start(copy):
        copy.start()

    def left(copy):
        copy.wait_send()

    def ag_row(part_, k):
        ag_copy(5 + 2 * k, part_, x, order[k], dev(xp, z, c), ag_r).start()
        ag_copy(6 + 2 * k, part_, x, order[k], dev(xm, z, c), ag_r).start()
        ag_copy(17 + k, part_, x, order[k], sib, ag_sib).start()

    def ag_col(part_, k):
        ag_wait(part_, x, order[k])
        ag_on(part_, k, start)
        ag_row(part_, k)

    def ag_near(part_, k):
        ag_wait(part_, xm, order[k])
        if k % 2 == 0:
            ag_copy(13 + k, part_, xm, order[k], dev(xp, z, c), ag_r).start()
        ag_copy(21 + k, part_, xm, order[k], sib, ag_sib).start()
        ag_wait(part_, xp, order[k])
        if k % 2 == 1:
            ag_copy(13 + k, part_, xp, order[k], dev(xm, z, c), ag_r).start()
        ag_copy(25 + k, part_, xp, order[k], sib, ag_sib).start()

    def ag_far(part_, k):
        ag_wait(part_, x2, order[k])
        ag_copy(29 + k, part_, x2, order[k], sib, ag_sib).start()

    def ag_own(part_):
        for x_ in range(4):
            for z_ in range(4):
                here = ag.at[(1 - c) * 16 + x_ * 4 + z_, PARTS[part_], :]
                at = part_ * 16 + x_ * 4 + z_
                send(here, here, ag_s.at[0], ag_sib.at[at], sib).wait_recv()

    ag_z(0, start)
    ag_row(0, 0)
    loop(1, N, lambda i: in_copy(lax.rem(t + i, N), t).start())
    hin[t] = tok_t[:, mine(t), :]
    ag_z(1, start)
    ag_row(1, 0)

    lanes = lax.broadcasted_iota(jnp.int32, (SUB, TOK), 1)
    subs = lax.broadcasted_iota(jnp.int32, (SUB, TOK), 0)
    pick = lanes == 4 * subs + (64 * c + x)
    window = 128 * lax.div(lax.rem(t, 8), 2)

    loads[4].wait()

    def factors(pr):
        where = pl.ds(pl.multiple_of(pr * CH + window, 128), 128)
        for j in range(4):
            for n in range(SEC):
                row = jnp.broadcast_to(angv[n, j : j + 1, where], (SUB, TOK))
                angle = jnp.sum(jnp.where(pick, row, 0.0), axis=1, keepdims=True)
                square = angle * angle
                inverse = 1.0 / (1.0 + square)
                ccos[n, pr, j] = jnp.broadcast_to((1.0 - square) * inverse, (SUB, TOK))
                csin[n, pr, j] = jnp.broadcast_to(2.0 * angle * inverse, (SUB, TOK))

    loop(0, 16, factors)
    loads[0].wait()
    dequantize(packk, ks, wk, 0, 1024)
    loads[1].wait()
    dequantize(packv, vs, wv, 0, 1024)

    loads[2].wait()
    dequantize(packq, qs, wq, 0, 2048)
    ag_col(0, 1)
    dequantize(packq, qs, wq, 2048, 2048)
    ag_near(0, 0)
    ag_col(0, 2)

    group(hin, s1, r1).wait_recv()

    def pair_of(n, pr):
        sh = 4 - n
        low = ((pr >> sh) << (sh + 1)) + (pr & ((1 << sh) - 1))
        return low, low + (1 << sh)

    def state(n, blk, j):
        if n == 0:
            return hin[blk, 0 if j < 3 else 1].astype(F32)
        return st[n - 1, blk, j].astype(F32)

    for n in range(SEC):

        def forward(pr, n=n):
            t0, t1 = pair_of(n, pr)
            for j in range(4):
                a, b = state(n, t0, j), state(n, t1, j)
                cs, sn = ccos[n, pr, j], csin[n, pr, j]
                low = (cs * a - sn * b).astype(BF16)
                high = (sn * a + cs * b).astype(BF16)
                if n < SEC - 1:
                    st[n, t0, j] = low
                    st[n, t1, j] = high
                else:
                    h5s[t0, j] = low
                    h5s[t1, j] = high

        loop(0, 16, forward)

    def h5_copy(p, src):
        return send(h5s.at[p], h5t.at[:, mine(src), :], s2.at[0], r2.at[0], p)


    ag_col(0, 3)
    ag_col(1, 1)
    loop(1, N, lambda i: h5_copy(lax.rem(t + i, N), t).start())
    h5t[:, mine(t), :] = h5s[t]
    ag_near(0, 1)
    dequantize(packq, qs, wq, 4096, 2048)
    ag_col(1, 2)
    ag_near(0, 2)
    ag_near(1, 0)
    dequantize(packq, qs, wq, 6144, 2048)
    ag_near(0, 3)
    ag_far(0, 0)
    ag_col(1, 3)
    ag_far(0, 1)
    ag_far(0, 2)
    ag_near(1, 1)
    ag_far(0, 3)

    def narrow(j, w, first):
        piece = dot(hl[j], w[...]).astype(BF16)
        for i in range(8):
            turned = dot_nt(eye(TOK), piece[:, 128 * i : 128 * i + 128]).astype(BF16)
            for k in range(4):
                slot = ((k % 2) * 4 + 2 * (i % 2) + k // 2) * 4 + i // 2
                part[slot, first : first + 32, :] = turned[32 * k : 32 * k + 32, :]

    def wide(zp):
        def column(x_):
            cols = pl.ds(pl.multiple_of((x_ * 4 + zp) * 512, 512), 512)
            for j, w, first in ((0, wq, 0), (3, wo, 320)):
                piece = dot(hl[j], w[:, cols]).astype(BF16)
                for c_ in range(2):
                    for half in range(2):
                        at = c_ * 256 + half * 128
                        rows = slice(first + half * 128, first + half * 128 + 128)
                        part[(c_ * 4 + zp) * 4 + x_, rows, :] = piece[:, at : at + 128]

        loop(0, 4, column)

    def piece_z(p):
        return (3, 0, 2, 1)[p]

    def base(zp):
        return (c * 4 + zp) * 4

    def a_copy(p):
        zp = piece_z(p)
        return send(
            part.at[pl.ds(((1 - c) * 4 + zp) * 4, 4)], ra.at[pl.ds(zp * 4, 4)],
            ra_s.at[p], ra_r.at[p], sib,
        )

    def x1_copy(p, way):
        zp = piece_z(p)
        return send(
            part.at[base(zp) + x2, pl.ds(way * HALF, HALF), :], rx1.at[zp, way],
            rx1_s.at[2 * p + way], rx1_r.at[2 * p + way], dev(xm if way else xp, z, c),
        )

    def x2_copy(p, way):
        zp = piece_z(p)
        to = xm if way else xp
        return send(
            part.at[base(zp) + to], rx2.at[zp, way],
            rx2_s.at[2 * p + way], rx2_r.at[2 * p + way], dev(to, z, c),
        )

    def z_copy(dest, src):
        return send(
            accx.at[dest], rz.at[src], rz_s.at[dest], rz_r.at[src], dev(x, dest, c)
        )

    def stage_z(dest):
        pl.when(z != dest)(lambda: z_copy(dest, z).start())

    def stage_x1(p):
        zp = piece_z(p)
        a_copy(p).wait_recv()
        add_rows(part, base(zp) + x2, (0, ROWS), [(ra, (zp * 4 + x2,), 0)])
        x1_copy(p, 0).start()
        x1_copy(p, 1).start()
        for x_ in (xp, xm, x):
            add_rows(part, base(zp) + x_, (0, ROWS), [(ra, (zp * 4 + x_,), 0)])

    def stage_x2(p):
        zp = piece_z(p)
        x1_copy(p, 0).wait_recv()
        add_rows(part, base(zp) + xp, (0, HALF), [(rx1, (zp, 0), 0)])
        x2_copy(p, 0).start()
        x1_copy(p, 1).wait_recv()
        add_rows(part, base(zp) + xm, (HALF, ROWS), [(rx1, (zp, 1), 0)])
        x2_copy(p, 1).start()

    def stage_x3(p):
        zp = piece_z(p)
        x2_copy(p, 0).wait_recv()
        x2_copy(p, 1).wait_recv()
        add_rows(part, base(zp) + x, (0, ROWS), [(rx2, (zp, 0), 0), (rx2, (zp, 1), 0)], accx, zp)

    def back_wide(j, w, first):
        total = None
        for quarter in range(4):
            rhs = jnp.concatenate(
                [
                    ag[c_ * 16 + 4 * quarter + i, first : first + 256, :]
                    for i in range(4)
                    for c_ in range(2)
                ],
                axis=0,
            )
            piece = dot(w[:, 2048 * quarter : 2048 * quarter + 2048], rhs)
            if quarter == 0:
                acc[...] = piece
            elif quarter < 3:
                acc[...] += piece
            else:
                bks[j] = (acc[...] + piece).astype(BF16)

    def back_narrow(j, w, first):
        rhs = jnp.concatenate(
            [ag[c_ * 16 + i, first : first + 32, :] for i in range(16) for c_ in range(2)], axis=0
        )
        bks[j] = dot(w[...], rhs).astype(BF16)

    def back_copy(k, p, slot):
        js = pl.ds(0, 3) if k == 0 else pl.ds(3, 1)
        return send(
            bks.at[js, mine(p), :], bkr.at[slot, js], s3.at[k], r3.at[k], p
        )

    ag_own(0)
    back_wide(0, wq, 0)
    back_narrow(1, wk, 256)
    back_narrow(2, wv, 288)
    loop(1, N, lambda i: back_copy(0, lax.rem(t + i, N), t).start())
    bkr[t, 0:3] = bks[0:3, mine(t), :]
    loads[3].wait()
    dequantize(packo, os_, wo, 0, 4096)
    ag_near(1, 2)
    ag_near(1, 3)
    ag_far(1, 0)
    dequantize(packo, os_, wo, 4096, 4096)

    group(h5s, s2, r2).wait_recv()
    for j in range(4):
        hl[j] = dot_nt(eye(TOK), h5t[j]).astype(BF16)
    narrow(1, wk, 256)
    narrow(2, wv, 288)
    wide(piece_z(0))
    a_copy(0).start()
    wide(piece_z(1))
    a_copy(1).start()
    stage_x1(0)
    for k in (1, 2, 3):
        ag_far(1, k)
    wide(piece_z(2))
    a_copy(2).start()
    stage_x1(1)
    ag_own(1)
    back_wide(3, wo, 320)
    loop(1, N, lambda i: back_copy(1, lax.rem(t + i, N), t).start())
    bkr[t, 3] = bks[3, mine(t), :]
    stage_x2(0)
    wide(piece_z(3))
    a_copy(3).start()
    stage_x1(2)
    stage_x2(1)

    def backward_sections(js):
        for n in reversed(range(SEC)):
            take, put = (bkr, gb) if n % 2 == 0 else (gb, bkr)

            def backward(pr, grads, n=n, take=take, put=put):
                t0, t1 = pair_of(n, pr)
                lows, highs = [], []
                for j in js:
                    cs, sn = ccos[n, pr, j], csin[n, pr, j]
                    gl, gu = take[t0, j].astype(F32), take[t1, j].astype(F32)
                    low = cs * gl + sn * gu
                    high = cs * gu - sn * gl
                    e = state(n, t0, j) * high - state(n, t1, j) * low
                    total = jnp.sum(e, axis=1, keepdims=True) * (1.0 + cs)
                    grads = jnp.where(lanes == pr * 4 + j, total, grads)
                    lows.append(low)
                    highs.append(high)
                    if n:
                        put[t0, j] = low.astype(BF16)
                        put[t1, j] = high.astype(BF16)
                if n == 0:
                    for blk, parts in ((t0, lows), (t1, highs)):
                        whole = parts[0] + parts[1] + parts[2] if len(js) == 3 else parts[0]
                        gs[0 if len(js) == 3 else 1, blk] = whole.astype(BF16)
                return grads

            first = jnp.zeros((SUB, TOK), F32) if len(js) == 3 else angy[y, n]
            angy[y, n] = lax.fori_loop(0, 16, backward, first, unroll=BU)

    def out_copy(k, p, src):
        return send(gs.at[k, p], gt.at[k, mine(src), :], s4.at[k], r4.at[k], p)

    group(bkr.at[:, pl.ds(0, 3)], s3, r3).wait_recv()
    backward_sections((0, 1, 2))
    loop(1, N, lambda i: out_copy(0, lax.rem(t + i, N), t).start())
    stage_x1(3)
    stage_x2(2)
    stage_x3(0)
    stage_z(piece_z(0))
    group(bkr.at[:, pl.ds(3, 1)], s3, r3, 1).wait_recv()
    backward_sections((3,))

    def y_copy(k, slot):
        return send(angy.at[slot], angy.at[slot], sd.at[k], rd.at[slot], dp_peers[k], "dp")

    for k in range(3):
        y_copy(k, y).start()

    loop(1, N, lambda i: out_copy(1, lax.rem(t + i, N), t).start())
    for k in range(2):
        gt[k, mine(t), :] = gs[k, t]
    stage_x2(3)
    stage_x3(1)
    stage_z(piece_z(1))

    def far_copy(slot):
        return send(angz.at[slot], angz.at[slot], sd.at[3], rd.at[4], far, "dp")

    stage_x3(2)
    stage_z(piece_z(2))
    for k in range(3):
        y_copy(k, lax.rem(y + 1 + k, 4)).wait_recv()
    for n in range(SEC):
        angz[zh, n] = ((angy[0, n] + angy[1, n]) + angy[2, n]) + angy[3, n]
    far_copy(zh).start()
    stage_x3(3)
    stage_z(piece_z(3))

    far_copy(1 - zh).wait_recv()
    for n in range(SEC):
        whole = angz[0, n] + angz[1, n]
        for pr in range(16):
            moved = pltpu.roll(whole, (4 * n - 4 * pr) % TOK, 1)
            keep = (lanes >= 4 * n) & (lanes < 4 * n + 4)
            spread[n, pr] = jnp.where(keep, moved, 0.0)

    def message(blk):
        whole = jnp.zeros((SUB, TOK), F32)
        for n in range(SEC):
            sh = 4 - n
            whole = whole + spread[n, ((blk >> (sh + 1)) << sh) + (blk & ((1 << sh) - 1))]
        top = whole.astype(BF16).astype(F32)
        rest = pltpu.roll(whole - top, 32, 1)
        angs[blk] = jnp.where(lanes < 32, top, rest).astype(BF16)

    def ang_copy(p, src):
        return send(angs.at[p], angt.at[mine(src), :], s5.at[0], r5.at[0], p)

    loop(0, N, message, unroll=4)
    loop(1, N, lambda i: ang_copy(lax.rem(t + i, N), t).start())
    angt[mine(t), :] = angs[t]

    total = accx[z].astype(F32)
    for k in (1, 2, 3):
        z_copy(0, order[k]).wait_recv()
    for k in (1, 2, 3):
        total = total + rz[order[k]].astype(F32)
    total = total.astype(BF16)
    q_out[:, 0:128] = total[0:128]
    q_out[:, 128:256] = total[128:256]
    o_out[:, 0:128] = total[320:448]
    o_out[:, 128:256] = total[448:576]
    k_out[...] = total[256:288]
    v_out[...] = total[288:320]

    def natural(value):
        return dot(dot_nt(eye(TOK), value).astype(BF16), perm[...])

    group(gs.at[0], s4, r4).wait_recv()
    tg[...] = natural(gt[0]).astype(BF16)
    group(gs.at[1], s4, r4, 1).wait_recv()
    mg[...] = natural(gt[1]).astype(BF16)

    group(hin, s1, r1).wait_send()
    group(h5s, s2, r2).wait_send()
    group(bkr.at[:, pl.ds(0, 3)], s3, r3).wait_send()
    group(bkr.at[:, pl.ds(3, 1)], s3, r3, 1).wait_send()
    group(gs.at[0], s4, r4).wait_send()
    group(gs.at[1], s4, r4, 1).wait_send()
    for part_ in range(2):
        ag_z(part_, left)
        for k in (1, 2, 3):
            ag_on(part_, k, left)
        loop(5, 33, lambda i, p=part_: ag_copy(i, p, x, z, sib, ag_r).wait_send())
    for p in range(4):
        a_copy(p).wait_send()
        for way in range(2):
            x1_copy(p, way).wait_send()
            x2_copy(p, way).wait_send()
        pl.when(z != p)(lambda p=p: z_copy(p, z).wait_send())
    for k in range(3):
        y_copy(k, y).wait_send()
    far_copy(zh).wait_send()

    group(angs, s5, r5).wait_recv()
    both = dot(dot_nt(eye(TOK)[0:64], angt[...]).astype(BF16), perm[...])
    ang_out[...] = both[0:32] + both[32:64]
    group(angs, s5, r5).wait_send()


def shards(*args):
    def vm(shape, dtype=BF16):
        return pltpu.VMEM(shape, dtype)

    def sem(n):
        return pltpu.SemaphoreType.DMA((n,))

    scratch = [
        vm((128, 8192), F32), vm((128, 1024), F32), vm((128, 1024), F32), vm((128, 8192), F32),
        vm((CH, 8192)), vm((CH, 1024)), vm((CH, 1024)), vm((CH, 8192)),
        vm((CH, CH)),
        vm((SEC, 4, 8192), F32), vm((2, CH, TOK)), vm((N, 2, SUB, TOK)),
        vm((SEC - 1, N, 4, SUB, TOK)), vm((N, 4, SUB, TOK)),
        vm((4, CH, TOK)), vm((4, TOK, CH)),
        vm((SEC, 16, 4, SUB, TOK), F32), vm((SEC, 16, 4, SUB, TOK), F32),
        vm((N, ROWS, TOK)), vm((N, ROWS, TOK)),
        vm((16, ROWS, TOK)),
        vm((4, 2, HALF, TOK)), vm((4, 2, ROWS, TOK)),
        vm((4, ROWS, TOK)), vm((4, ROWS, TOK)),
        vm((CH, TOK), F32),
        vm((4, CH, TOK)), vm((N, 4, SUB, TOK)), vm((N, 4, SUB, TOK)),
        vm((2, N, SUB, TOK)), vm((2, CH, TOK)),
        vm((4, SEC, SUB, TOK), F32), vm((2, SEC, SUB, TOK), F32),
        vm((SEC, 16, SUB, TOK), F32), vm((N, SUB, TOK)), vm((CH, TOK)),
        sem(5), sem(1), sem(1), sem(1), sem(1), sem(2), sem(2), sem(2), sem(2),
        sem(66), sem(32), sem(32), sem(4), sem(4), sem(8), sem(8), sem(8), sem(8),
        sem(4), sem(4), sem(4), sem(5), sem(1), sem(1),
    ]
    shapes = [(TOK, 256), (32, TOK), (32, TOK), (TOK, 256), (TOK, CH), (TOK, CH)]
    outs = [jax.ShapeDtypeStruct(shape, BF16) for shape in shapes]
    in_vmem = pl.BlockSpec(memory_space=pltpu.VMEM)
    in_any = pl.BlockSpec(memory_space=pl.ANY)
    args = list(args)
    args[2] = args[2].transpose(1, 0, 2)
    args[12], args[13] = args[12].T, args[13].T
    results = pl.pallas_call(
        kernel,
        out_shape=outs + [jax.ShapeDtypeStruct((32, CH), F32)],
        in_specs=[in_any if i in (2, 3, 5, 7, 9) else in_vmem for i in range(15)],
        out_specs=[in_vmem] * 7,
        scratch_shapes=scratch,
        compiler_params=pltpu.CompilerParams(
            collective_id=0, has_side_effects=True, vmem_limit_bytes=62 * 1024 * 1024
        ),
        cost_estimate=pl.CostEstimate(
            flops=4 * TOK * CH * 18432, bytes_accessed=12_000_000, transcendentals=0
        ),
    )(*args)

    def hand_over(*refs):
        for src, dst in zip(refs[:6], refs[7:13]):
            dst[...] = src[...]
        for n in range(SEC):
            refs[13][n] = refs[6][4 * n : 4 * n + 4, :]

    final = pl.pallas_call(
        hand_over,
        out_shape=outs + [jax.ShapeDtypeStruct((SEC, 4, CH), F32)],
        in_specs=[in_vmem] * 7,
        out_specs=[in_vmem] * 7,
    )(*results)
    q_out, k_out, v_out, o_out, tg, mg, ang = final
    return q_out, k_out.T, v_out.T, o_out, tg, mg, ang.transpose(1, 0, 2)


def solution(mesh):
    both = P("dp", "tensor")
    rows = P("tensor", None)
    return jax.shard_map(
        shards,
        mesh=mesh,
        in_specs=(both, both, P(), rows, rows, rows, rows, rows, rows, rows, rows)
        + (both, both, both, both),
        out_specs=(both, both, both, both, both, both, P(None, None, "tensor")),
        check_vma=False,
    )
```

```python
import jax
import jax.numpy as jnp
from jax import lax
from jax.experimental import pallas as pl
from jax.experimental.pallas import tpu as pltpu
from jax.sharding import PartitionSpec as P

F32 = jnp.float32
BF16 = jnp.bfloat16
MESH = pl.DeviceIdType.MESH
N = 32
BU = 4
CH = 512
SUB = 16
TOK = 128
SEC = 5
ROWS = 576
HALF = 288
PARTS = (pl.ds(0, 320), pl.ds(320, 256))
NT = (((1,), (1,)), ((), ()))


def dot(a, b):
    return jnp.dot(a, b, preferred_element_type=F32)


def dot_nt(a, b):
    return lax.dot_general(a, b, NT, preferred_element_type=F32)


def eye(n):
    r = lax.broadcasted_iota(jnp.int32, (n, n), 0)
    c = lax.broadcasted_iota(jnp.int32, (n, n), 1)
    return jnp.where(r == c, 1.0, 0.0).astype(BF16)


def loop(lo, hi, fn, unroll=1):
    def step(i, carry):
        fn(i)
        return carry

    lax.fori_loop(lo, hi, step, 0, unroll=unroll)


def dequantize(packed, scale, out, first, width):
    def chunk(i):
        cols = pl.ds(pl.multiple_of(first + i * 128, 128), 128)
        spread = scale[:, cols].astype(F32)
        for g in range(8):
            rows = slice(16 * g, 16 * g + 16)
            word = packed[rows, cols].astype(jnp.int32)
            s = jnp.broadcast_to(spread[g : g + 1, :], (16, 128))
            for plane in range(4):
                digit = (word >> (4 * plane)) & 15 if plane < 3 else word >> 12
                value = (digit.astype(F32) - 7.5) * s
                out[128 * plane + 16 * g : 128 * plane + 16 * g + 16, cols] = value.astype(BF16)

    loop(0, width // 128, chunk)


def add_rows(dst, base, rows, srcs, out=None, out_base=0):
    def step(i):
        off = pl.multiple_of(i * 96, 96)
        total = dst[base, pl.ds(rows[0] + off, 96), :].astype(F32)
        for ref, index, first in srcs:
            total = total + ref[index + (pl.ds(first + off, 96), slice(None))].astype(F32)
        if out is None:
            dst[base, pl.ds(rows[0] + off, 96), :] = total.astype(BF16)
        else:
            out[out_base, pl.ds(rows[0] + off, 96), :] = total.astype(BF16)

    loop(0, (rows[1] - rows[0]) // 96, step)


def kernel(
    tok, mix, ang, qp, qs, kp, ks, vp, vs, op, os_, qc, kc, vc, oc,
    q_out, k_out, v_out, o_out, tg, mg, ang_out,
    packq, packk, packv, packo, wq, wk, wv, wo, perm,
    angv, tok_t, hin, st, h5s, h5t, hl, ccos, csin,
    ag, part, ra, rx1, rx2, accx, rz, acc, bks, bkr, gb, gs, gt, angy, angz, spread, angs, angt,
    ld, s1, r1, s2, r2, s3, r3, s4, r4, ag_s, ag_r, ag_sib, ra_s, ra_r, rx1_s, rx1_r,
    rx2_s, rx2_r, rz_s, rz_r, sd, rd, s5, r5,
):
    d = lax.axis_index("dp")
    t = lax.axis_index("tensor")
    x = lax.div(t, 8)
    z = lax.rem(lax.div(t, 2), 4)
    c = lax.rem(t, 2)
    xp, xm, x2 = lax.rem(x + 1, 4), lax.rem(x + 3, 4), lax.rem(x + 2, 4)

    def dev(x_, z_, c_):
        return (x_ * 4 + z_) * 2 + c_

    sib = dev(x, z, 1 - c)
    y, zh = lax.div(d, 2), lax.rem(d, 2)
    far = y * 2 + 1 - zh
    dp_peers = [lax.rem(y + i, 4) * 2 + zh for i in (1, 2, 3)] + [far]

    def send(src, dst, ssem, rsem, peer, axis="tensor"):
        return pltpu.make_async_remote_copy(
            src_ref=src, dst_ref=dst, send_sem=ssem, recv_sem=rsem,
            device_id={axis: peer}, device_id_type=MESH,
        )

    bar = pltpu.get_barrier_semaphore()
    loop(1, N, lambda i: pl.semaphore_signal(
        bar, inc=1, device_id={"tensor": lax.rem(t + i, N)}, device_id_type=MESH))
    for peer in dp_peers:
        pl.semaphore_signal(bar, inc=1, device_id={"dp": peer}, device_id_type=MESH)

    loads = [
        pltpu.make_async_copy(src, dst, ld.at[i])
        for i, (src, dst) in enumerate(((kp, packk), (vp, packv), (qp, packq), (op, packo), (ang, angv)))
    ]
    for i in (4, 0, 1, 2, 3):
        loads[i].start()
    r = lax.broadcasted_iota(jnp.int32, (CH, CH), 0)
    col = lax.broadcasted_iota(jnp.int32, (CH, CH), 1)
    perm[...] = jnp.where(col == 4 * (r & 127) + (r >> 7), 1.0, 0.0).astype(BF16)
    tok_t[0] = dot_nt(perm[...], tok[...]).astype(BF16)
    tok_t[1] = dot_nt(perm[...], mix[...]).astype(BF16)
    own = c * 16 + x * 4 + z
    ag[own, 0:256, :] = dot_nt(eye(256), qc[...]).astype(BF16)
    ag[own, 320:576, :] = dot_nt(eye(256), oc[...]).astype(BF16)
    ag[own, 256:288, :] = kc[...]
    ag[own, 288:320, :] = vc[...]
    pl.semaphore_wait(bar, N - 1 + 4)

    def mine(p):
        return pl.ds(pl.multiple_of(p * SUB, SUB), SUB)

    def group(ref, ssem, rsem, k=0):
        all_ = ref.at[pl.ds(0, N - 1)]
        return send(all_, all_, ssem.at[k], rsem.at[k], sib)

    def in_copy(p, slot):
        return send(tok_t.at[:, mine(p), :], hin.at[slot], s1.at[0], r1.at[0], p)

    near = z - 1 + 2 * lax.div(3 - z, 3)
    last = 3 * (1 - lax.div(z, 2))
    order = (z, near, 6 - z - near - last, last)

    def ag_copy(k, part_, x_, z_, peer, sems):
        here = ag.at[c * 16 + x_ * 4 + z_, PARTS[part_], :]
        at = part_ * 16 + x_ * 4 + z_
        return send(here, here, ag_s.at[part_ * 33 + k], sems.at[at], peer)

    def ag_wait(part_, x_, z_):
        ag_copy(0, part_, x_, z_, sib, ag_r).wait_recv()

    def upward(part_, k, z_):
        return ag_copy(k, part_, x, z_, dev(x, z + 1, c), ag_r)

    def downward(part_, k, z_):
        return ag_copy(k, part_, x, z_, dev(x, z - 1, c), ag_r)

    def ag_z(part_, act):
        @pl.when(z < 3)
        def _():
            act(upward(part_, 0, z))

        @pl.when(z > 0)
        def _():
            act(downward(part_, 1, z))

    def ag_on(part_, k, act):
        @pl.when((order[k] < z) & (z < 3))
        def _():
            act(upward(part_, 1 + k, order[k]))

        @pl.when((order[k] > z) & (z > 0))
        def _():
            act(downward(part_, 1 + k, order[k]))

    def start(copy):
        copy.start()

    def left(copy):
        copy.wait_send()

    def ag_row(part_, k):
        ag_copy(5 + 2 * k, part_, x, order[k], dev(xp, z, c), ag_r).start()
        ag_copy(6 + 2 * k, part_, x, order[k], dev(xm, z, c), ag_r).start()
        ag_copy(17 + k, part_, x, order[k], sib, ag_sib).start()

    def ag_col(part_, k):
        ag_wait(part_, x, order[k])
        ag_on(part_, k, start)
        ag_row(part_, k)

    def ag_near(part_, k):
        ag_wait(part_, xm, order[k])
        if k % 2 == 0:
            ag_copy(13 + k, part_, xm, order[k], dev(xp, z, c), ag_r).start()
        ag_copy(21 + k, part_, xm, order[k], sib, ag_sib).start()
        ag_wait(part_, xp, order[k])
        if k % 2 == 1:
            ag_copy(13 + k, part_, xp, order[k], dev(xm, z, c), ag_r).start()
        ag_copy(25 + k, part_, xp, order[k], sib, ag_sib).start()

    def ag_far(part_, k):
        ag_wait(part_, x2, order[k])
        ag_copy(29 + k, part_, x2, order[k], sib, ag_sib).start()

    def ag_own(part_):
        for x_ in range(4):
            for z_ in range(4):
                here = ag.at[(1 - c) * 16 + x_ * 4 + z_, PARTS[part_], :]
                at = part_ * 16 + x_ * 4 + z_
                send(here, here, ag_s.at[0], ag_sib.at[at], sib).wait_recv()

    ag_z(0, start)
    ag_row(0, 0)
    loop(1, N, lambda i: in_copy(lax.rem(t + i, N), t).start())
    hin[t] = tok_t[:, mine(t), :]
    ag_z(1, start)
    ag_row(1, 0)

    lanes = lax.broadcasted_iota(jnp.int32, (SUB, TOK), 1)
    subs = lax.broadcasted_iota(jnp.int32, (SUB, TOK), 0)
    pick = lanes == 4 * subs + (64 * c + x)
    window = 128 * lax.div(lax.rem(t, 8), 2)

    loads[4].wait()

    def factors(pr):
        where = pl.ds(pl.multiple_of(pr * CH + window, 128), 128)
        for j in range(4):
            for n in range(SEC):
                row = jnp.broadcast_to(angv[n, j : j + 1, where], (SUB, TOK))
                angle = jnp.sum(jnp.where(pick, row, 0.0), axis=1, keepdims=True)
                square = angle * angle
                inverse = 1.0 / (1.0 + square)
                ccos[n, pr, j] = jnp.broadcast_to((1.0 - square) * inverse, (SUB, TOK))
                csin[n, pr, j] = jnp.broadcast_to(2.0 * angle * inverse, (SUB, TOK))

    loop(0, 16, factors)
    loads[0].wait()
    dequantize(packk, ks, wk, 0, 1024)
    loads[1].wait()
    dequantize(packv, vs, wv, 0, 1024)

    loads[2].wait()
    dequantize(packq, qs, wq, 0, 2048)
    ag_col(0, 1)
    dequantize(packq, qs, wq, 2048, 2048)
    ag_near(0, 0)
    ag_col(0, 2)

    group(hin, s1, r1).wait_recv()

    def pair_of(n, pr):
        sh = 4 - n
        low = ((pr >> sh) << (sh + 1)) + (pr & ((1 << sh) - 1))
        return low, low + (1 << sh)

    def state(n, blk, j):
        if n == 0:
            return hin[blk, 0 if j < 3 else 1].astype(F32)
        return st[n - 1, blk, j].astype(F32)

    for n in range(SEC):

        def forward(pr, n=n):
            t0, t1 = pair_of(n, pr)
            for j in range(4):
                a, b = state(n, t0, j), state(n, t1, j)
                cs, sn = ccos[n, pr, j], csin[n, pr, j]
                low = (cs * a - sn * b).astype(BF16)
                high = (sn * a + cs * b).astype(BF16)
                if n < SEC - 1:
                    st[n, t0, j] = low
                    st[n, t1, j] = high
                else:
                    h5s[t0, j] = low
                    h5s[t1, j] = high

        loop(0, 16, forward)

    def h5_copy(p, src):
        return send(h5s.at[p], h5t.at[:, mine(src), :], s2.at[0], r2.at[0], p)


    ag_col(0, 3)
    ag_col(1, 1)
    loop(1, N, lambda i: h5_copy(lax.rem(t + i, N), t).start())
    h5t[:, mine(t), :] = h5s[t]
    ag_near(0, 1)
    dequantize(packq, qs, wq, 4096, 2048)
    ag_col(1, 2)
    ag_near(0, 2)
    ag_near(1, 0)
    dequantize(packq, qs, wq, 6144, 2048)
    ag_near(0, 3)
    ag_far(0, 0)
    ag_col(1, 3)
    ag_far(0, 1)
    ag_far(0, 2)
    ag_near(1, 1)
    ag_far(0, 3)

    def narrow(j, w, first):
        piece = dot(hl[j], w[...]).astype(BF16)
        for i in range(8):
            turned = dot_nt(eye(TOK), piece[:, 128 * i : 128 * i + 128]).astype(BF16)
            for k in range(4):
                slot = ((k % 2) * 4 + 2 * (i % 2) + k // 2) * 4 + i // 2
                part[slot, first : first + 32, :] = turned[32 * k : 32 * k + 32, :]

    def wide(zp):
        def column(x_):
            cols = pl.ds(pl.multiple_of((x_ * 4 + zp) * 512, 512), 512)
            for j, w, first in ((0, wq, 0), (3, wo, 320)):
                piece = dot(hl[j], w[:, cols]).astype(BF16)
                for c_ in range(2):
                    for half in range(2):
                        at = c_ * 256 + half * 128
                        rows = slice(first + half * 128, first + half * 128 + 128)
                        part[(c_ * 4 + zp) * 4 + x_, rows, :] = piece[:, at : at + 128]

        loop(0, 4, column)

    def piece_z(p):
        return (3, 0, 2, 1)[p]

    def base(zp):
        return (c * 4 + zp) * 4

    def a_copy(p):
        zp = piece_z(p)
        return send(
            part.at[pl.ds(((1 - c) * 4 + zp) * 4, 4)], ra.at[pl.ds(zp * 4, 4)],
            ra_s.at[p], ra_r.at[p], sib,
        )

    def x1_copy(p, way):
        zp = piece_z(p)
        return send(
            part.at[base(zp) + x2, pl.ds(way * HALF, HALF), :], rx1.at[zp, way],
            rx1_s.at[2 * p + way], rx1_r.at[2 * p + way], dev(xm if way else xp, z, c),
        )

    def x2_copy(p, way):
        zp = piece_z(p)
        to = xm if way else xp
        return send(
            part.at[base(zp) + to], rx2.at[zp, way],
            rx2_s.at[2 * p + way], rx2_r.at[2 * p + way], dev(to, z, c),
        )

    def z_copy(dest, src):
        return send(
            accx.at[dest], rz.at[src], rz_s.at[dest], rz_r.at[src], dev(x, dest, c)
        )

    def stage_z(dest):
        pl.when(z != dest)(lambda: z_copy(dest, z).start())

    def stage_x1(p):
        zp = piece_z(p)
        a_copy(p).wait_recv()
        add_rows(part, base(zp) + x2, (0, ROWS), [(ra, (zp * 4 + x2,), 0)])
        x1_copy(p, 0).start()
        x1_copy(p, 1).start()
        for x_ in (xp, xm, x):
            add_rows(part, base(zp) + x_, (0, ROWS), [(ra, (zp * 4 + x_,), 0)])

    def stage_x2(p):
        zp = piece_z(p)
        x1_copy(p, 0).wait_recv()
        add_rows(part, base(zp) + xp, (0, HALF), [(rx1, (zp, 0), 0)])
        x2_copy(p, 0).start()
        x1_copy(p, 1).wait_recv()
        add_rows(part, base(zp) + xm, (HALF, ROWS), [(rx1, (zp, 1), 0)])
        x2_copy(p, 1).start()

    def stage_x3(p):
        zp = piece_z(p)
        x2_copy(p, 0).wait_recv()
        x2_copy(p, 1).wait_recv()
        add_rows(part, base(zp) + x, (0, ROWS), [(rx2, (zp, 0), 0), (rx2, (zp, 1), 0)], accx, zp)

    def back_wide(j, w, first):
        total = None
        for quarter in range(4):
            rhs = jnp.concatenate(
                [
                    ag[c_ * 16 + 4 * quarter + i, first : first + 256, :]
                    for i in range(4)
                    for c_ in range(2)
                ],
                axis=0,
            )
            piece = dot(w[:, 2048 * quarter : 2048 * quarter + 2048], rhs)
            if quarter == 0:
                acc[...] = piece
            elif quarter < 3:
                acc[...] += piece
            else:
                bks[j] = (acc[...] + piece).astype(BF16)

    def back_narrow(j, w, first):
        rhs = jnp.concatenate(
            [ag[c_ * 16 + i, first : first + 32, :] for i in range(16) for c_ in range(2)], axis=0
        )
        bks[j] = dot(w[...], rhs).astype(BF16)

    def back_copy(k, p, slot):
        js = pl.ds(0, 3) if k == 0 else pl.ds(3, 1)
        return send(
            bks.at[js, mine(p), :], bkr.at[slot, js], s3.at[k], r3.at[k], p
        )

    ag_own(0)
    back_wide(0, wq, 0)
    back_narrow(1, wk, 256)
    back_narrow(2, wv, 288)
    loop(1, N, lambda i: back_copy(0, lax.rem(t + i, N), t).start())
    bkr[t, 0:3] = bks[0:3, mine(t), :]
    loads[3].wait()
    dequantize(packo, os_, wo, 0, 4096)
    ag_near(1, 2)
    ag_near(1, 3)
    ag_far(1, 0)
    dequantize(packo, os_, wo, 4096, 4096)

    group(h5s, s2, r2).wait_recv()
    for j in range(4):
        hl[j] = dot_nt(eye(TOK), h5t[j]).astype(BF16)
    narrow(1, wk, 256)
    narrow(2, wv, 288)
    wide(piece_z(0))
    a_copy(0).start()
    wide(piece_z(1))
    a_copy(1).start()
    stage_x1(0)
    for k in (1, 2, 3):
        ag_far(1, k)
    wide(piece_z(2))
    a_copy(2).start()
    stage_x1(1)
    ag_own(1)
    back_wide(3, wo, 320)
    loop(1, N, lambda i: back_copy(1, lax.rem(t + i, N), t).start())
    bkr[t, 3] = bks[3, mine(t), :]
    stage_x2(0)
    wide(piece_z(3))
    a_copy(3).start()
    stage_x1(2)
    stage_x2(1)

    def backward_sections(js):
        for n in reversed(range(SEC)):
            take, put = (bkr, gb) if n % 2 == 0 else (gb, bkr)

            def backward(pr, grads, n=n, take=take, put=put):
                t0, t1 = pair_of(n, pr)
                lows, highs = [], []
                for j in js:
                    cs, sn = ccos[n, pr, j], csin[n, pr, j]
                    gl, gu = take[t0, j].astype(F32), take[t1, j].astype(F32)
                    low = cs * gl + sn * gu
                    high = cs * gu - sn * gl
                    e = state(n, t0, j) * high - state(n, t1, j) * low
                    total = jnp.sum(e, axis=1, keepdims=True) * (1.0 + cs)
                    grads = jnp.where(lanes == pr * 4 + j, total, grads)
                    lows.append(low)
                    highs.append(high)
                    if n:
                        put[t0, j] = low.astype(BF16)
                        put[t1, j] = high.astype(BF16)
                if n == 0:
                    for blk, parts in ((t0, lows), (t1, highs)):
                        whole = parts[0] + parts[1] + parts[2] if len(js) == 3 else parts[0]
                        gs[0 if len(js) == 3 else 1, blk] = whole.astype(BF16)
                return grads

            first = jnp.zeros((SUB, TOK), F32) if len(js) == 3 else angy[y, n]
            angy[y, n] = lax.fori_loop(0, 16, backward, first, unroll=BU)

    def out_copy(k, p, src):
        return send(gs.at[k, p], gt.at[k, mine(src), :], s4.at[k], r4.at[k], p)

    group(bkr.at[:, pl.ds(0, 3)], s3, r3).wait_recv()
    backward_sections((0, 1, 2))
    loop(1, N, lambda i: out_copy(0, lax.rem(t + i, N), t).start())
    stage_x1(3)
    stage_x2(2)
    stage_x3(0)
    stage_z(piece_z(0))
    group(bkr.at[:, pl.ds(3, 1)], s3, r3, 1).wait_recv()
    backward_sections((3,))

    def y_copy(k, slot):
        return send(angy.at[slot], angy.at[slot], sd.at[k], rd.at[slot], dp_peers[k], "dp")

    for k in range(3):
        y_copy(k, y).start()

    loop(1, N, lambda i: out_copy(1, lax.rem(t + i, N), t).start())
    for k in range(2):
        gt[k, mine(t), :] = gs[k, t]
    stage_x2(3)
    stage_x3(1)
    stage_z(piece_z(1))

    def far_copy(slot):
        return send(angz.at[slot], angz.at[slot], sd.at[3], rd.at[4], far, "dp")

    for k in range(3):
        y_copy(k, lax.rem(y + 1 + k, 4)).wait_recv()
    for n in range(SEC):
        angz[zh, n] = ((angy[0, n] + angy[1, n]) + angy[2, n]) + angy[3, n]
    far_copy(zh).start()
    stage_x3(2)
    stage_z(piece_z(2))
    stage_x3(3)
    stage_z(piece_z(3))

    far_copy(1 - zh).wait_recv()
    for n in range(SEC):
        whole = angz[0, n] + angz[1, n]
        for pr in range(16):
            moved = pltpu.roll(whole, (4 * n - 4 * pr) % TOK, 1)
            keep = (lanes >= 4 * n) & (lanes < 4 * n + 4)
            spread[n, pr] = jnp.where(keep, moved, 0.0)

    def message(blk):
        whole = jnp.zeros((SUB, TOK), F32)
        for n in range(SEC):
            sh = 4 - n
            whole = whole + spread[n, ((blk >> (sh + 1)) << sh) + (blk & ((1 << sh) - 1))]
        top = whole.astype(BF16).astype(F32)
        rest = pltpu.roll(whole - top, 32, 1)
        angs[blk] = jnp.where(lanes < 32, top, rest).astype(BF16)

    def ang_copy(p, src):
        return send(angs.at[p], angt.at[mine(src), :], s5.at[0], r5.at[0], p)

    loop(0, N, message, unroll=4)
    loop(1, N, lambda i: ang_copy(lax.rem(t + i, N), t).start())
    angt[mine(t), :] = angs[t]

    total = accx[z].astype(F32)
    for k in (1, 2, 3):
        z_copy(0, order[k]).wait_recv()
    for k in (1, 2, 3):
        total = total + rz[order[k]].astype(F32)
    total = total.astype(BF16)
    q_out[:, 0:128] = total[0:128]
    q_out[:, 128:256] = total[128:256]
    o_out[:, 0:128] = total[320:448]
    o_out[:, 128:256] = total[448:576]
    k_out[...] = total[256:288]
    v_out[...] = total[288:320]

    def natural(value):
        return dot(dot_nt(eye(TOK), value).astype(BF16), perm[...])

    group(gs.at[0], s4, r4).wait_recv()
    tg[...] = natural(gt[0]).astype(BF16)
    group(gs.at[1], s4, r4, 1).wait_recv()
    mg[...] = natural(gt[1]).astype(BF16)

    group(hin, s1, r1).wait_send()
    group(h5s, s2, r2).wait_send()
    group(bkr.at[:, pl.ds(0, 3)], s3, r3).wait_send()
    group(bkr.at[:, pl.ds(3, 1)], s3, r3, 1).wait_send()
    group(gs.at[0], s4, r4).wait_send()
    group(gs.at[1], s4, r4, 1).wait_send()
    for part_ in range(2):
        ag_z(part_, left)
        for k in (1, 2, 3):
            ag_on(part_, k, left)
        loop(5, 33, lambda i, p=part_: ag_copy(i, p, x, z, sib, ag_r).wait_send())
    for p in range(4):
        a_copy(p).wait_send()
        for way in range(2):
            x1_copy(p, way).wait_send()
            x2_copy(p, way).wait_send()
        pl.when(z != p)(lambda p=p: z_copy(p, z).wait_send())
    for k in range(3):
        y_copy(k, y).wait_send()
    far_copy(zh).wait_send()

    group(angs, s5, r5).wait_recv()
    both = dot(dot_nt(eye(TOK)[0:64], angt[...]).astype(BF16), perm[...])
    ang_out[...] = both[0:32] + both[32:64]
    group(angs, s5, r5).wait_send()


def shards(*args):
    def vm(shape, dtype=BF16):
        return pltpu.VMEM(shape, dtype)

    def sem(n):
        return pltpu.SemaphoreType.DMA((n,))

    scratch = [
        vm((128, 8192), F32), vm((128, 1024), F32), vm((128, 1024), F32), vm((128, 8192), F32),
        vm((CH, 8192)), vm((CH, 1024)), vm((CH, 1024)), vm((CH, 8192)),
        vm((CH, CH)),
        vm((SEC, 4, 8192), F32), vm((2, CH, TOK)), vm((N, 2, SUB, TOK)),
        vm((SEC - 1, N, 4, SUB, TOK)), vm((N, 4, SUB, TOK)),
        vm((4, CH, TOK)), vm((4, TOK, CH)),
        vm((SEC, 16, 4, SUB, TOK), F32), vm((SEC, 16, 4, SUB, TOK), F32),
        vm((N, ROWS, TOK)), vm((N, ROWS, TOK)),
        vm((16, ROWS, TOK)),
        vm((4, 2, HALF, TOK)), vm((4, 2, ROWS, TOK)),
        vm((4, ROWS, TOK)), vm((4, ROWS, TOK)),
        vm((CH, TOK), F32),
        vm((4, CH, TOK)), vm((N, 4, SUB, TOK)), vm((N, 4, SUB, TOK)),
        vm((2, N, SUB, TOK)), vm((2, CH, TOK)),
        vm((4, SEC, SUB, TOK), F32), vm((2, SEC, SUB, TOK), F32),
        vm((SEC, 16, SUB, TOK), F32), vm((N, SUB, TOK)), vm((CH, TOK)),
        sem(5), sem(1), sem(1), sem(1), sem(1), sem(2), sem(2), sem(2), sem(2),
        sem(66), sem(32), sem(32), sem(4), sem(4), sem(8), sem(8), sem(8), sem(8),
        sem(4), sem(4), sem(4), sem(5), sem(1), sem(1),
    ]
    shapes = [(TOK, 256), (32, TOK), (32, TOK), (TOK, 256), (TOK, CH), (TOK, CH)]
    outs = [jax.ShapeDtypeStruct(shape, BF16) for shape in shapes]
    in_vmem = pl.BlockSpec(memory_space=pltpu.VMEM)
    in_any = pl.BlockSpec(memory_space=pl.ANY)
    args = list(args)
    args[2] = args[2].transpose(1, 0, 2)
    args[12], args[13] = args[12].T, args[13].T
    results = pl.pallas_call(
        kernel,
        out_shape=outs + [jax.ShapeDtypeStruct((32, CH), F32)],
        in_specs=[in_any if i in (2, 3, 5, 7, 9) else in_vmem for i in range(15)],
        out_specs=[in_vmem] * 7,
        scratch_shapes=scratch,
        compiler_params=pltpu.CompilerParams(
            collective_id=0, has_side_effects=True, vmem_limit_bytes=62 * 1024 * 1024
        ),
        cost_estimate=pl.CostEstimate(
            flops=4 * TOK * CH * 18432, bytes_accessed=12_000_000, transcendentals=0
        ),
    )(*args)

    def hand_over(*refs):
        for src, dst in zip(refs[:6], refs[7:13]):
            dst[...] = src[...]
        for n in range(SEC):
            refs[13][n] = refs[6][4 * n : 4 * n + 4, :]

    final = pl.pallas_call(
        hand_over,
        out_shape=outs + [jax.ShapeDtypeStruct((SEC, 4, CH), F32)],
        in_specs=[in_vmem] * 7,
        out_specs=[in_vmem] * 7,
    )(*results)
    q_out, k_out, v_out, o_out, tg, mg, ang = final
    return q_out, k_out.T, v_out.T, o_out, tg, mg, ang.transpose(1, 0, 2)


def solution(mesh):
    both = P("dp", "tensor")
    rows = P("tensor", None)
    return jax.shard_map(
        shards,
        mesh=mesh,
        in_specs=(both, both, P(), rows, rows, rows, rows, rows, rows, rows, rows)
        + (both, both, both, both),
        out_specs=(both, both, both, both, both, both, P(None, None, "tensor")),
        check_vma=False,
    )
```
